256 devices in a mesh: wave: 8 (over x_lo, y), slab: 32 (over x_hi, z, core).
Axes of the slice: x: 4 (x_hi: 2, x_lo: 2; x = x_hi * 2 + x_lo), y: 4, z: 8, core: 2. Of those that a mesh axis runs over, the one named last changes fastest.
Arguments:
- levels: int32 [2048, 2048], P('slab', 'wave'), may hold values from 0 to 15
- offsets: float32 [2048, 2048], P('slab', 'wave'), may hold values from -0.3 to 0.3
- targets: int32 [8, 64, 2], replicated, may hold values from 0 to 2047
- w_in: float32 [256], replicated, may hold values from -96 to 96
- b_in: float32 [256], replicated, may hold values from -87 to 87
- w_out: bfloat16 [256, 16], replicated, may hold values from -0.046875 to 0.046875
- b_out: float32 [16], replicated, may hold values from -2 to 2
Outputs:
- width_gradient: float32 [2048, 2048], P('slab', 'wave')
The draws below stay inside these ranges and needn't reach their ends.
All inputs are finite; a program needn't handle non-finite values.
Results may differ from the reference program's by a relative error of at most 0.0039.
Values may be sent and summed in bfloat16 or wider, within the bound.
No kernel may reach another device: no remote copies, remote signals or barrier semaphores. Data moves between devices by JAX's collectives and lax.ppermute only.
A program may use at most 64 MiB of HBM per device.

```python
import math
import jax
import jax.numpy as jnp
from jax import lax

N = 2048
UNITS = 256
SPOTS = 64
LEVELS = 16
WAVES = 8
FOCAL = 128
SPOT_LEVEL = 256


def pillar_units(key, slope_low, slope_high, place_low, place_high):
    sign_key, size_key, place_key = jax.random.split(jax.random.fold_in(key, 11), 3)
    signs = jnp.where(jax.random.bernoulli(sign_key, 0.5, (UNITS,)), 1.0, -1.0).astype(jnp.float32)
    fraction = jax.random.uniform(size_key, (UNITS,), jnp.float32, 0.0, 1.0)
    magnitude = slope_low * jnp.exp(fraction * math.log(slope_high / slope_low))
    places = jax.random.uniform(place_key, (UNITS,), jnp.float32, place_low, place_high)
    slopes = signs * magnitude
    return (slopes, -slopes * places)


def draw_w_in(key, part):
    slopes, biases = pillar_units(key, 32.0, 96.0, 0.1, 0.9)
    return slopes


def draw_b_in(key, part):
    slopes, biases = pillar_units(key, 32.0, 96.0, 0.1, 0.9)
    return biases


def place_ends(array, rng, least, high):
    longest = array.shape.index(max(array.shape))
    spots = []
    for shift in (0, 1):
        where = [jax.random.randint(jax.random.fold_in(rng, axis), (), 0, length) for axis, length in enumerate(array.shape)]
        where[longest] = (where[longest] + shift) % array.shape[longest]
        spots.append(tuple(where))
    return array.at[spots[0]].set(least).at[spots[1]].set(high)


def steps_of(rng, extent, cuts, low, largest):
    level = 1.0
    for dim, parts in cuts:
        steps = jax.random.uniform(jax.random.fold_in(jax.random.fold_in(rng, 6), dim), (parts,), jnp.float32, low / len(cuts), largest / len(cuts))
        level = level * jnp.repeat(jnp.exp(steps), extent[dim] // parts).reshape((-1,) + (1,) * (len(extent) - 1 - dim))
    return level


def noise(key, dims, spread, limit, cuts=(), held_as=jnp.bfloat16):
    array = jax.random.normal(key, dims, jnp.float32) * spread
    if len(cuts) > 0:
        array = steps_of(key, dims, cuts, -0.22, 0.18) * array
    return jnp.clip(array, min=-limit, max=limit).astype(held_as)


def setup_inputs(seed: int = 0) -> dict:
    seeds = jax.random.split(jax.random.key(seed), 8)
    return {
        "levels": place_ends(jax.random.randint(seeds[0], (N, N), 0, LEVELS), jax.random.fold_in(seeds[0], 1), 0, LEVELS - 1).astype(jnp.int32),
        "offsets": noise(seeds[1], (N, N), 0.1, 0.3, ((0, 32), (1, 8)), jnp.float32),
        "targets": place_ends(jax.random.randint(seeds[2], (WAVES, SPOTS, 2), 0, N), jax.random.fold_in(seeds[2], 1), 0, N - 1).astype(jnp.int32),
        "w_in": draw_w_in(jax.random.fold_in(seeds[7], 71), 0),
        "b_in": draw_b_in(jax.random.fold_in(seeds[7], 71), 0),
        "w_out": noise(seeds[5], (UNITS, 2 * WAVES), (UNITS * 64) ** -0.5, 0.046875),
        "b_out": noise(seeds[6], (2 * WAVES,), 0.5, 2.0, (), jnp.float32),
    }


def level_widths(levels, offsets):
    return 0.3 + levels.astype(jnp.float32) * (0.4 / (LEVELS - 1)) + offsets

def surrogate(widths, w_in, b_in, w_out, b_out):
    pre_act = widths[..., None] * w_in + b_in
    hidden = (pre_act * jax.nn.sigmoid(pre_act)).astype(jnp.bfloat16)
    mixed_out = jnp.einsum('rch,hj->jrc', hidden.astype(jnp.float32), w_out.astype(jnp.float32))
    return (mixed_out + b_out[:, None, None]).astype(jnp.bfloat16)

def width_slope(widths, w_in, b_in, w_out, cotangent):
    pre_act = widths[..., None] * w_in + b_in
    sigmoid_value = jax.nn.sigmoid(pre_act)
    back_hidden = jnp.einsum('jrc,hj->rch', cotangent.astype(jnp.float32), w_out.astype(jnp.float32))
    act_slope = sigmoid_value * (1.0 + pre_act * (1.0 - sigmoid_value))
    return lax.optimization_barrier(jnp.sum(back_hidden * act_slope * w_in, axis=-1))

def frequencies(length, first_index, total_len):
    index_all = first_index + jnp.arange(length, dtype=jnp.int32)
    signed_index = jnp.where(index_all < total_len // 2, index_all, index_all - total_len)
    return signed_index.astype(jnp.float32) * (2.0 * math.pi / total_len)

def transfer(wavelength, kx_rows, ky_cols, focal_length):
    wave_number = 2.0 * math.pi / wavelength
    kz_square = wave_number * wave_number - kx_rows[:, None] ** 2 - ky_cols[None, :] ** 2
    kz_root = jnp.sqrt(jnp.abs(kz_square))
    is_open = kz_square > 0.0
    phase_angle = jnp.where(is_open, focal_length * kz_root, 0.0)
    amplitude = jnp.where(is_open, 1.0, jnp.exp(-focal_length * kz_root))
    return (amplitude * jnp.cos(phase_angle), amplitude * jnp.sin(phase_angle))

def reference(levels, offsets, targets, w_in, b_in, w_out, b_out):
    block_rows = min(N, 64)
    count_blocks = N // block_rows
    widths = level_widths(levels, offsets)

    def forward_block(width_rows):
        return surrogate(width_rows, w_in, b_in, w_out, b_out)
    transmission = lax.map(forward_block, widths.reshape(count_blocks, block_rows, N))
    transmission = jnp.transpose(transmission, (1, 0, 2, 3)).reshape(2 * WAVES, N, N)
    kx_all = frequencies(N, 0, N)

    def per_wave(wave_index):
        wavelength = 1.5 + wave_index.astype(jnp.float32) / (WAVES - 1)
        kern_re, kern_im = transfer(wavelength, kx_all, kx_all, float(FOCAL))
        kernel = lax.complex(kern_re, kern_im)
        source = lax.complex(transmission[wave_index].astype(jnp.float32), transmission[WAVES + wave_index].astype(jnp.float32))
        focal_field = jnp.fft.ifft2(kernel * jnp.fft.fft2(source))
        intensity = focal_field.real ** 2 + focal_field.imag ** 2
        own_targets = targets[wave_index]
        spot_map = jnp.zeros((N, N), jnp.float32).at[own_targets[:, 0], own_targets[:, 1]].add(float(SPOT_LEVEL))
        adjoint = (intensity - spot_map) * focal_field / WAVES
        back_field = jnp.fft.ifft2(jnp.conj(kernel) * jnp.fft.fft2(adjoint))
        return jnp.stack([back_field.real, back_field.imag]).astype(jnp.bfloat16)
    cotangent = lax.map(per_wave, jnp.arange(WAVES, dtype=jnp.int32))
    cotangent = jnp.transpose(cotangent, (1, 0, 2, 3)).reshape(2 * WAVES, count_blocks, block_rows, N)
    cotangent = jnp.transpose(cotangent, (1, 0, 2, 3))

    def backward_block(pieces):
        return width_slope(pieces[0], w_in, b_in, w_out, pieces[1])
    gradient = lax.map(backward_block, (widths.reshape(count_blocks, block_rows, N), cotangent))
    return gradient.reshape(N, N)
```

```python
import math

import jax
import jax.numpy as jnp
import ml_dtypes
import numpy as np
from jax import lax
from jax.experimental import pallas as pl
from jax.experimental.pallas import tpu as pltpu
from jax.sharding import Mesh, PartitionSpec as P


LEVELS = 16
WAVES = 8
SIDE = 2048
FIRST = 32
SECOND = 64
LANES = 2 * SECOND
SLAB = ("xh", "z", "c")
WAVE = ("xl", "y")
PLANE = ("xl", "y", "xh", "c")
VMEM_LIMIT = 48 * 2**20


def split_np(table):
    high = table.astype(np.float32).astype(ml_dtypes.bfloat16)
    low = (table - high.astype(np.float64)).astype(np.float32).astype(ml_dtypes.bfloat16)
    return high, low


def row_tables(direction):
    angle = direction * 2.0 * math.pi / SECOND * (np.arange(SECOND)[:, None] * np.arange(SECOND)[None, :] % SECOND)
    scale = 1.0 if direction < 0 else 1.0 / SIDE
    cos, sin = np.cos(angle) * scale, np.sin(angle) * scale
    high, low = split_np(np.block([[cos, sin], [-sin, cos]]))
    return np.block([[high, low], [high, np.zeros_like(low)]])


def row_twiddles():
    angle = -2.0 * math.pi / SIDE * (np.arange(FIRST)[:, None] * np.arange(SECOND)[None, :])
    cos, sin = np.cos(angle), np.sin(angle)
    return np.stack([np.concatenate([cos, cos], 1), np.concatenate([-sin, sin], 1)], 1).astype(np.float32)


def col_tables(direction):
    place = np.arange(SECOND)
    freq = np.arange(FIRST)[:, None] + FIRST * place[None, :]
    index = freq[:, :, None] * place[None, None, :] % SIDE
    if direction > 0:
        index = np.transpose(index, (0, 2, 1))
    scale = 1.0 if direction < 0 else 1.0 / SIDE
    angle = direction * 2.0 * math.pi / SIDE * index
    table = np.concatenate([np.cos(angle) * scale, np.sin(angle) * scale], 2)
    high, low = split_np(table)
    if direction > 0:
        return np.concatenate([high, low], 1)
    return np.concatenate(
        [np.concatenate([high, high], 2), np.concatenate([low, np.zeros_like(low)], 2)], 1
    )


def lane_signs():
    lane = lax.broadcasted_iota(jnp.int32, (1, LANES), 1)
    return jnp.where(lane < SECOND, -1.0, 1.0).astype(jnp.float32)


def swap(x):
    return pltpu.roll(x, SECOND, x.ndim - 1)


def dft32(parts, direction, signs):
    count = len(parts)
    if count == 1:
        return parts
    even = dft32(parts[0::2], direction, signs)
    odd = dft32(parts[1::2], direction, signs)
    half = count // 2
    lower, upper = [], []
    for k in range(half):
        if k == 0:
            turned = odd[k]
        elif 2 * k == half:
            turned = swap(odd[k]) * (direction * signs)
        else:
            angle = direction * 2.0 * math.pi * k / count
            turned = odd[k] * math.cos(angle) + swap(odd[k]) * (signs * math.sin(angle))
        lower.append(even[k] + turned)
        upper.append(even[k] - turned)
    return lower + upper


def split_pair(x):
    high = x.astype(jnp.bfloat16)
    return high, (x - high.astype(jnp.float32)).astype(jnp.bfloat16)


def matmul(left, right):
    return jnp.dot(left, right, preferred_element_type=jnp.float32)


def col_forward_step(y_ref, w_ref, out_ref, signs, k):
    part = y_ref[k]
    high, low = split_pair(jnp.concatenate([part, swap(part) * signs], 0))
    both = matmul(w_ref[k], jnp.concatenate([high, low], 0))
    out_ref[k] = (both[:SECOND] + both[SECOND:]).astype(jnp.bfloat16)


def col_inverse_step(x_ref, v_ref, y_ref, signs, k):
    part = x_ref[k].astype(jnp.float32)
    data = jnp.concatenate([part, swap(part) * signs], 0).astype(jnp.bfloat16)
    both = matmul(v_ref[k], data)
    y_ref[k] = both[:SECOND] + both[SECOND:]


def col_first_kernel(x_ref, c_ref, w_ref, out_ref, y_ref):
    signs = lane_signs()
    mean = c_ref[0:1, :]
    for g in range(0, SECOND, 16):
        block = [x_ref[a, g : g + 16, :].astype(jnp.float32) - mean for a in range(FIRST)]
        for h in (0, 8):
            for k, part in enumerate(dft32([b[h : h + 8] for b in block], -1.0, signs)):
                y_ref[k, g + h : g + h + 8, :] = part
    for k in range(FIRST):
        col_forward_step(y_ref, w_ref, out_ref, signs, k)


def col_middle_kernel(x_ref, c_ref, s_ref, v_ref, w_ref, out_ref, y_ref):
    signs = lane_signs()
    back = c_ref[1:2, :]
    mean = c_ref[2:3, :]
    for k in range(FIRST):
        col_inverse_step(x_ref, v_ref, y_ref, signs, k)
    for g in range(0, SECOND, 8):
        rows = slice(g, g + 8)
        field = dft32([y_ref[k, rows, :] for k in range(FIRST)], 1.0, signs)
        adjoint = []
        for a in range(FIRST):
            value = field[a] + back
            square = value * value
            weight = (square + swap(square) - s_ref[a, rows, :]) * (1.0 / WAVES)
            adjoint.append(weight * value - mean)
        for k, part in enumerate(dft32(adjoint, -1.0, signs)):
            y_ref[k, rows, :] = part
    for k in range(FIRST):
        col_forward_step(y_ref, w_ref, out_ref, signs, k)


def col_last_kernel(x_ref, c_ref, v_ref, out_ref, y_ref):
    signs = lane_signs()
    back = c_ref[3:4, :]
    for k in range(FIRST):
        col_inverse_step(x_ref, v_ref, y_ref, signs, k)
    for g in range(0, SECOND, 16):
        halves = []
        for h in (0, 8):
            halves.append(dft32([y_ref[k, g + h : g + h + 8, :] for k in range(FIRST)], 1.0, signs))
        for a in range(FIRST):
            whole = jnp.concatenate([halves[0][a], halves[1][a]], 0) + back
            out_ref[a, g : g + 16, :] = whole.astype(jnp.bfloat16)


def row_kernel(x_ref, kr_ref, ki_ref, t_ref, w_ref, v_ref, out_ref, y_ref):
    signs = lane_signs()
    for g in range(0, SECOND, 16):
        block = [x_ref[a, g : g + 16, :].astype(jnp.float32) for a in range(FIRST)]
        for h in (0, 8):
            for k, part in enumerate(dft32([b[h : h + 8] for b in block], -1.0, signs)):
                y_ref[k, g + h : g + h + 8, :] = part * t_ref[k, 0:1, :] + swap(part) * t_ref[k, 1:2, :]
    step = 4
    rows = step * SECOND
    for k in range(0, FIRST, step):
        high, low = split_pair(y_ref[k : k + step].reshape(rows, LANES))
        both = matmul(jnp.concatenate([high, low], 1), w_ref[...])
        freq = both[:, :LANES] + both[:, LANES:]
        kr = kr_ref[k : k + step].reshape(rows, LANES)
        ki = ki_ref[k : k + step].reshape(rows, LANES)
        high, low = split_pair(freq * kr + swap(freq) * ki)
        both = matmul(jnp.concatenate([high, low], 1), v_ref[...])
        place = both[:, :LANES] + both[:, LANES:]
        turned = swap(place)
        for i in range(step):
            part = slice(i * SECOND, (i + 1) * SECOND)
            y_ref[k + i] = place[part] * t_ref[k + i, 0:1, :] - turned[part] * t_ref[k + i, 1:2, :]
    for g in range(0, SECOND, 16):
        halves = []
        for h in (0, 8):
            halves.append(dft32([y_ref[k, g + h : g + h + 8, :] for k in range(FIRST)], 1.0, signs))
        for a in range(FIRST):
            out_ref[a, g : g + 16, :] = jnp.concatenate([halves[0][a], halves[1][a]], 0).astype(jnp.bfloat16)


def pack_kernel(x_ref, out_ref):
    lane = lax.broadcasted_iota(jnp.int32, (1, LANES), 1)
    left = lane < SECOND
    for w in range(WAVES):
        for tile in range(2):
            real = x_ref[w, :, tile * LANES : (tile + 1) * LANES].astype(jnp.float32)
            imag = x_ref[WAVES + w, :, tile * LANES : (tile + 1) * LANES].astype(jnp.float32)
            place = tile * 2 * WAVES + w * 2
            out_ref[place] = jnp.where(left, real, swap(imag)).astype(out_ref.dtype)
            out_ref[place + 1] = jnp.where(left, swap(real), imag).astype(out_ref.dtype)


def combine_kernel(x_ref, d_ref, out_ref):
    lane = lax.broadcasted_iota(jnp.int32, (1, LANES), 1)
    left = lane < SECOND
    for tile in range(2):
        sums = []
        for core in range(2):
            total = None
            for w in range(WAVES):
                place = tile * 2 * WAVES + w * 2 + core
                term = x_ref[place].astype(jnp.float32) * d_ref[place]
                total = term if total is None else total + term
            sums.append(total + swap(total))
        out_ref[:, tile * LANES : (tile + 1) * LANES] = jnp.where(left, sums[0], sums[1])


def call(kernel, out_shape, *args, scratch=True, flops=10**8, name=None):
    size = sum(a.size * a.dtype.itemsize for a in args) + math.prod(out_shape.shape) * out_shape.dtype.itemsize
    return pl.pallas_call(
        kernel,
        out_shape=out_shape,
        scratch_shapes=[pltpu.VMEM((FIRST, SECOND, LANES), jnp.float32)] if scratch else [],
        compiler_params=pltpu.CompilerParams(vmem_limit_bytes=VMEM_LIMIT),
        cost_estimate=pl.CostEstimate(flops=flops, bytes_accessed=size, transcendentals=0),
        name=name,
    )(*args)


def level_widths(levels, offsets):
    return 0.3 + levels.astype(jnp.float32) * (0.4 / (LEVELS - 1)) + offsets


def surrogate_rows(widths, w_in, b_in, w_out, b_out):
    pre_act = widths[..., None] * w_in + b_in
    hidden = (pre_act * jax.nn.sigmoid(pre_act)).astype(jnp.bfloat16)
    mixed_out = (
        jnp.einsum("rch,hj->jrc", hidden, w_out, preferred_element_type=jnp.float32) + b_out[:, None, None]
    )
    return mixed_out.astype(jnp.bfloat16)


def slope_rows(widths, w_in, b_in, w_out):
    pre_act = widths[..., None] * w_in + b_in
    gate = jax.nn.sigmoid(pre_act)
    slope = gate * (1.0 + pre_act * (1.0 - gate)) * w_in
    return jnp.einsum("rch,hj->jrc", slope.astype(jnp.bfloat16), w_out, preferred_element_type=jnp.float32)


def signed_kappa(index):
    signed = jnp.where(index < SIDE // 2, index, index - SIDE)
    return signed.astype(jnp.float32) * (2.0 * math.pi / SIDE)


def transfer(wavelength, kx, ky, focal_length):
    wave_number = 2.0 * math.pi / wavelength
    kz_square = wave_number * wave_number - kx**2 - ky**2
    kz_root = jnp.sqrt(jnp.abs(kz_square))
    is_open = kz_square > 0.0
    phase_angle = jnp.where(is_open, focal_length * kz_root, 0.0)
    amplitude = jnp.where(is_open, 1.0, jnp.exp(-focal_length * kz_root))
    return (amplitude * jnp.cos(phase_angle), amplitude * jnp.sin(phase_angle))


def usual_transmission(w_in, b_in, w_out, b_out):
    nodes, weights = np.polynomial.hermite_e.hermegauss(8)
    weights = weights / weights.sum()
    shifts = np.clip(0.1 * nodes, -0.3, 0.3)
    places = (0.3 + 0.4 * np.arange(LEVELS)[:, None] / (LEVELS - 1) + shifts[None, :]).reshape(-1)
    shares = np.tile(weights / LEVELS, LEVELS).astype(np.float32)
    pre_act = places.astype(np.float32)[:, None] * w_in[None, :] + b_in[None, :]
    hidden = pre_act * jax.nn.sigmoid(pre_act)
    values = jnp.dot(hidden, w_out.astype(jnp.float32)) + b_out
    mean = jnp.sum(values * shares[:, None], 0)
    spread = jnp.sum((values - mean) ** 2 * shares[:, None], 0)
    return mean, spread


def lanes_pair(real, imag):
    return jnp.concatenate([jnp.full((1, SECOND), real), jnp.full((1, SECOND), imag)], 1)


def local(levels, offsets, targets, w_in, b_in, w_out, b_out):
    block = (FIRST, SECOND, LANES)
    packed16 = jax.ShapeDtypeStruct(block, jnp.bfloat16)
    packed32 = jax.ShapeDtypeStruct(block, jnp.float32)
    wave_index = lax.axis_index("z")
    plane_index = lax.axis_index(PLANE)
    wavelength = 1.5 + wave_index.astype(jnp.float32) / (WAVES - 1)
    focal_length = float(SIDE // 16)
    spot_level = float(SIDE // 8)
    col_forward = jnp.asarray(col_tables(-1.0))
    col_inverse = jnp.asarray(col_tables(1.0))
    row_forward = jnp.asarray(row_tables(-1.0))
    row_inverse = jnp.asarray(row_tables(1.0))
    twiddles = jnp.asarray(row_twiddles())

    widths = level_widths(levels, offsets)
    trans = surrogate_rows(widths, w_in, b_in, w_out, b_out)
    sent = call(pack_kernel, packed16, trans, scratch=False, name="pack")
    cols = lax.all_to_all(sent, SLAB, 0, 0, tiled=True)

    mean, spread = usual_transmission(w_in, b_in, w_out, b_out)
    mean_re = lax.dynamic_index_in_dim(mean, wave_index, 0, keepdims=False)
    mean_im = lax.dynamic_index_in_dim(mean, wave_index + WAVES, 0, keepdims=False)
    noise = lax.dynamic_index_in_dim(spread, wave_index, 0, keepdims=False) + lax.dynamic_index_in_dim(
        spread, wave_index + WAVES, 0, keepdims=False
    )
    zero = jnp.zeros((), jnp.float32)
    dc_re, dc_im = transfer(wavelength, zero, zero, focal_length)
    field_re = mean_re * dc_re - mean_im * dc_im
    field_im = mean_re * dc_im + mean_im * dc_re
    spots_mean = spot_level * targets.shape[1] / (SIDE * SIDE)
    gain = (field_re * field_re + field_im * field_im + 2.0 * noise - spots_mean) / WAVES
    adj_re = gain * field_re
    adj_im = gain * field_im
    back_re = adj_re * dc_re + adj_im * dc_im
    back_im = adj_im * dc_re - adj_re * dc_im
    consts = jnp.concatenate(
        [
            lanes_pair(mean_re, mean_im),
            lanes_pair(field_re, field_im),
            lanes_pair(adj_re, adj_im),
            lanes_pair(back_re, back_im),
            jnp.zeros((4, LANES), jnp.float32),
        ],
        0,
    )

    second = jnp.arange(SECOND, dtype=jnp.int32)
    kx = signed_kappa(plane_index + FIRST * second)
    ky = signed_kappa(jnp.arange(FIRST, dtype=jnp.int32)[:, None] + FIRST * second[None, :])
    kern_re, kern_im = transfer(wavelength, kx[None, :, None], ky[:, None, :], focal_length)
    kr = jnp.concatenate([kern_re, kern_re], 2)
    ki = jnp.concatenate([-kern_im, kern_im], 2)
    ki_conj = -ki

    own_targets = lax.dynamic_index_in_dim(targets, wave_index, 0, keepdims=False)
    row_hit = (own_targets[:, 0][None, :] == jnp.arange(SIDE, dtype=jnp.int32)[:, None]).astype(jnp.bfloat16)
    lane_cols = plane_index * SECOND + jnp.arange(LANES, dtype=jnp.int32) % SECOND
    col_hit = (own_targets[:, 1][:, None] == lane_cols[None, :]).astype(jnp.bfloat16)
    spots = (spot_level * jnp.dot(row_hit, col_hit, preferred_element_type=jnp.float32)).reshape(block)

    slopes = call(pack_kernel, packed32, slope_rows(widths, w_in, b_in, w_out), scratch=False, name="pack_slopes")

    def exchange(x):
        return lax.all_to_all(x, PLANE, 0, 0, tiled=True)

    rows = exchange(call(col_first_kernel, packed16, cols, consts, col_forward, name="col_first"))
    rows = call(row_kernel, packed16, rows, kr, ki, twiddles, row_forward, row_inverse, name="row_one")
    cols = exchange(rows)
    cols = call(col_middle_kernel, packed16, cols, consts, spots, col_inverse, col_forward, name="col_middle")
    rows = exchange(cols)
    rows = call(row_kernel, packed16, rows, kr, ki_conj, twiddles, row_forward, row_inverse, name="row_two")
    cols = exchange(rows)
    cotangent = call(col_last_kernel, packed16, cols, consts, col_inverse, name="col_last")
    returned = lax.all_to_all(cotangent, SLAB, 0, 0, tiled=True)
    return call(
        combine_kernel, jax.ShapeDtypeStruct(levels.shape, jnp.float32), returned, slopes, scratch=False, name="combine"
    )


def solution(mesh):
    fine = Mesh(mesh.devices.reshape(2, 4, 2, 8, 2), ("xl", "y", "xh", "z", "c"))
    placed = (P(SLAB, WAVE), P(SLAB, WAVE), P(), P(), P(), P(), P())
    return jax.shard_map(local, mesh=fine, in_specs=placed, out_specs=P(SLAB, WAVE), check_vma=False)
```

```python
import functools
import math

import jax
import jax.numpy as jnp
import ml_dtypes
import numpy as np
from jax import lax
from jax.experimental import pallas as pl
from jax.experimental.pallas import tpu as pltpu
from jax.sharding import Mesh, PartitionSpec as P


LEVELS = 16
WAVES = 8
SIDE = 2048
FIRST = 32
SECOND = 64
LANES = 2 * SECOND
ROWS = SECOND // 2
SLAB = ("xh", "z", "c")
WAVE = ("xl", "y")
PLANE = ("xl", "y", "xh", "c")
VMEM_LIMIT = 16 * 2**20


def split_np(table):
    high = table.astype(np.float32).astype(ml_dtypes.bfloat16)
    low = (table - high.astype(np.float64)).astype(np.float32).astype(ml_dtypes.bfloat16)
    return high, low


def small_dft(direction):
    place = np.arange(SECOND)
    angle = direction * 2.0 * math.pi / SECOND * (place[:, None] * place[None, :] % SECOND)
    scale = 1.0 if direction < 0 else 1.0 / SIDE
    return np.cos(angle) * scale, np.sin(angle) * scale


def row_tables(direction):
    cos, sin = small_dft(direction)
    pair = np.eye(2)
    table = np.block([[np.kron(pair, cos), np.kron(pair, sin)], [-np.kron(pair, sin), np.kron(pair, cos)]])
    high, low = split_np(table)
    return np.concatenate([high, high, low], 0)


def col_tables(direction):
    cos, sin = small_dft(direction)
    halves = []
    for cut in (slice(0, ROWS), slice(ROWS, SECOND)):
        halves.append((np.concatenate([cos[:, cut], -sin[:, cut]], 1), np.concatenate([sin[:, cut], cos[:, cut]], 1)))
    high, low = split_np(np.concatenate([halves[0][0], halves[1][0], halves[0][1], halves[1][1]], 0))
    return np.concatenate([high, high, low] if direction < 0 else [high, low], 1)


def row_twiddles():
    angle = -2.0 * math.pi / SIDE * (np.arange(FIRST)[:, None] * np.arange(SECOND)[None, :])
    return np.stack([np.tile(np.cos(angle), (1, 2)), np.tile(np.sin(angle), (1, 2))], 1).astype(np.float32)


def col_twiddles():
    place = np.arange(ROWS)[:, None] + ROWS * (np.arange(LANES) // SECOND)[None, :]
    angle = -2.0 * math.pi / SIDE * (np.arange(FIRST)[:, None, None] * place[None])
    return np.stack([np.cos(angle), np.sin(angle)]).astype(np.float32)


def left_lanes():
    return lax.broadcasted_iota(jnp.int32, (1, LANES), 1) < SECOND


def swap(x):
    return pltpu.roll(x, SECOND, x.ndim - 1)


def dft(real, imag, direction):
    count = len(real)
    if count == 1:
        return real, imag
    even_re, even_im = dft(real[0::2], imag[0::2], direction)
    odd_re, odd_im = dft(real[1::2], imag[1::2], direction)
    half = count // 2
    lower_re, lower_im, upper_re, upper_im = [], [], [], []
    for k in range(half):
        a, b = odd_re[k], odd_im[k]
        if k == 0:
            turn_re, turn_im = a, b
        elif 2 * k == half:
            turn_re, turn_im = (b, -a) if direction < 0 else (-b, a)
        else:
            angle = direction * 2.0 * math.pi * k / count
            cos, sin = math.cos(angle), math.sin(angle)
            turn_re, turn_im = a * cos - b * sin, a * sin + b * cos
        lower_re.append(even_re[k] + turn_re)
        lower_im.append(even_im[k] + turn_im)
        upper_re.append(even_re[k] - turn_re)
        upper_im.append(even_im[k] - turn_im)
    return lower_re + upper_re, lower_im + upper_im


def split_pair(x):
    high = x.astype(jnp.bfloat16)
    return high, (x - high.astype(jnp.float32)).astype(jnp.bfloat16)


def matmul(left, right):
    return jnp.dot(left, right, preferred_element_type=jnp.float32)


def load_groups(x_ref, g):
    real = [x_ref[a, g : g + 16, :].astype(jnp.float32) for a in range(FIRST)]
    imag = [x_ref[a, ROWS + g : ROWS + g + 16, :].astype(jnp.float32) for a in range(FIRST)]
    return [([r[h : h + 8] for r in real], [i[h : h + 8] for i in imag]) for h in (0, 8)]


def store_groups(out_ref, g, halves):
    for part in range(2):
        for a in range(FIRST):
            whole = jnp.concatenate([halves[0][part][a], halves[1][part][a]], 0)
            out_ref[a, part * ROWS + g : part * ROWS + g + 16, :] = whole.astype(jnp.bfloat16)


def join_halves(both):
    left = left_lanes()
    parts = []
    for first in (0, 2 * SECOND):
        low, high = both[first : first + SECOND], both[first + SECOND : first + 2 * SECOND]
        base = jnp.where(left, low[:ROWS], high[ROWS:])
        moved = jnp.where(left, low[ROWS:], high[:ROWS])
        parts.append(base + swap(moved))
    return parts


def col_forward(y_ref, w_ref, out_ref):
    for k in range(0, FIRST, 2):
        data = [jnp.concatenate([y_ref[0, k + i], y_ref[1, k + i]], 0) for i in range(2)]
        high, low = split_pair(jnp.concatenate(data, 1))
        both = matmul(w_ref[...], jnp.concatenate([high, low, high], 0))
        for i in range(2):
            real, imag = join_halves(both[:, i * LANES : (i + 1) * LANES])
            out_ref[k + i] = jnp.concatenate([real, imag], 0).astype(jnp.bfloat16)


def col_inverse(x_ref, v_ref, t_ref, y_ref):
    for k in range(0, FIRST, 2):
        data = jnp.concatenate([x_ref[k], x_ref[k + 1]], 1)
        both = matmul(v_ref[...], jnp.concatenate([data, data], 0))
        for i in range(2):
            real, imag = join_halves(both[:, i * LANES : (i + 1) * LANES])
            cos, sin = t_ref[0, k + i], t_ref[1, k + i]
            y_ref[0, k + i] = real * cos + imag * sin
            y_ref[1, k + i] = imag * cos - real * sin


def turn_and_keep(y_ref, t_ref, rows, real, imag):
    for k in range(FIRST):
        cos, sin = t_ref[0, k, rows, :], t_ref[1, k, rows, :]
        y_ref[0, k, rows, :] = real[k] * cos - imag[k] * sin
        y_ref[1, k, rows, :] = real[k] * sin + imag[k] * cos


def col_first_kernel(x_ref, c_ref, t_ref, w_ref, out_ref, y_ref):
    mean_re, mean_im = c_ref[0:1, :], c_ref[1:2, :]
    for g in range(0, ROWS, 16):
        for h, (real, imag) in enumerate(load_groups(x_ref, g)):
            real, imag = dft([r - mean_re for r in real], [i - mean_im for i in imag], -1.0)
            turn_and_keep(y_ref, t_ref, slice(g + 8 * h, g + 8 * h + 8), real, imag)
    col_forward(y_ref, w_ref, out_ref)


def col_middle_kernel(x_ref, c_ref, s_ref, t_ref, v_ref, w_ref, out_ref, y_ref):
    field_re, field_im = c_ref[2:3, :], c_ref[3:4, :]
    mean_re, mean_im = c_ref[4:5, :], c_ref[5:6, :]
    col_inverse(x_ref, v_ref, t_ref, y_ref)
    for g in range(0, ROWS, 8):
        rows = slice(g, g + 8)
        real, imag = dft(
            [y_ref[0, k, rows, :] for k in range(FIRST)], [y_ref[1, k, rows, :] for k in range(FIRST)], 1.0
        )
        for a in range(FIRST):
            value_re, value_im = real[a] + field_re, imag[a] + field_im
            weight = (value_re * value_re + value_im * value_im - s_ref[a, rows, :]) * (1.0 / WAVES)
            real[a] = weight * value_re - mean_re
            imag[a] = weight * value_im - mean_im
        real, imag = dft(real, imag, -1.0)
        turn_and_keep(y_ref, t_ref, rows, real, imag)
    col_forward(y_ref, w_ref, out_ref)


def col_last_kernel(x_ref, c_ref, t_ref, v_ref, out_ref, y_ref):
    back_re, back_im = c_ref[6:7, :], c_ref[7:8, :]
    col_inverse(x_ref, v_ref, t_ref, y_ref)
    for g in range(0, ROWS, 16):
        halves = []
        for h in (0, 8):
            rows = slice(g + h, g + h + 8)
            real, imag = dft(
                [y_ref[0, k, rows, :] for k in range(FIRST)], [y_ref[1, k, rows, :] for k in range(FIRST)], 1.0
            )
            halves.append(([r + back_re for r in real], [i + back_im for i in imag]))
        store_groups(out_ref, g, halves)


def row_step(real, imag, w_ref):
    high, low = split_pair(jnp.concatenate([real, imag], 1))
    both = matmul(jnp.concatenate([high, low, high], 1), w_ref[...])
    return both[:, :LANES], both[:, LANES:]


def row_kernel(conjugate, x_ref, kr_ref, ki_ref, t_ref, w_ref, v_ref, out_ref, y_ref):
    for g in range(0, ROWS, 16):
        for h, (real, imag) in enumerate(load_groups(x_ref, g)):
            real, imag = dft(real, imag, -1.0)
            rows = slice(g + 8 * h, g + 8 * h + 8)
            for k in range(FIRST):
                cos, sin = t_ref[k, 0:1, :], t_ref[k, 1:2, :]
                y_ref[0, k, rows, :] = real[k] * cos - imag[k] * sin
                y_ref[1, k, rows, :] = real[k] * sin + imag[k] * cos
    step = 8
    rows = step * ROWS
    for k in range(0, FIRST, step):
        real, imag = row_step(
            y_ref[0, k : k + step].reshape(rows, LANES), y_ref[1, k : k + step].reshape(rows, LANES), w_ref
        )
        kr = kr_ref[k : k + step].reshape(rows, LANES)
        ki = ki_ref[k : k + step].reshape(rows, LANES)
        if conjugate:
            real, imag = real * kr + imag * ki, imag * kr - real * ki
        else:
            real, imag = real * kr - imag * ki, imag * kr + real * ki
        real, imag = row_step(real, imag, v_ref)
        for i in range(step):
            part = slice(i * ROWS, (i + 1) * ROWS)
            cos, sin = t_ref[k + i, 0:1, :], t_ref[k + i, 1:2, :]
            y_ref[0, k + i] = real[part] * cos + imag[part] * sin
            y_ref[1, k + i] = imag[part] * cos - real[part] * sin
    for g in range(0, ROWS, 16):
        halves = []
        for h in (0, 8):
            rows = slice(g + h, g + h + 8)
            halves.append(
                dft([y_ref[0, k, rows, :] for k in range(FIRST)], [y_ref[1, k, rows, :] for k in range(FIRST)], 1.0)
            )
        store_groups(out_ref, g, halves)


def pack_kernel(x_ref, out_ref):
    left = left_lanes()
    for w in range(WAVES):
        for tile in range(2):
            lanes = slice(tile * LANES, (tile + 1) * LANES)
            place = tile * 2 * WAVES + w * 2
            for part in range(2):
                whole = x_ref[part * WAVES + w, :, lanes].astype(jnp.float32)
                top, low = whole[:ROWS], whole[ROWS:]
                rows = slice(part * ROWS, (part + 1) * ROWS)
                out_ref[place, rows, :] = jnp.where(left, top, swap(low)).astype(out_ref.dtype)
                out_ref[place + 1, rows, :] = jnp.where(left, swap(top), low).astype(out_ref.dtype)


def combine_kernel(x_ref, d_ref, out_ref):
    left = left_lanes()
    for tile in range(2):
        sums = []
        for core in range(2):
            total = None
            for w in range(WAVES):
                place = tile * 2 * WAVES + w * 2 + core
                term = x_ref[place].astype(jnp.float32) * d_ref[place]
                total = term if total is None else total + term
            sums.append(total[:ROWS] + total[ROWS:])
        lanes = slice(tile * LANES, (tile + 1) * LANES)
        out_ref[:ROWS, lanes] = jnp.where(left, sums[0], swap(sums[1]))
        out_ref[ROWS:, lanes] = jnp.where(left, swap(sums[0]), sums[1])


def call(kernel, out_shape, *args, scratch=True, flops=10**8, name=None):
    size = sum(a.size * a.dtype.itemsize for a in args) + math.prod(out_shape.shape) * out_shape.dtype.itemsize
    return pl.pallas_call(
        kernel,
        out_shape=out_shape,
        scratch_shapes=[pltpu.VMEM((2, FIRST, ROWS, LANES), jnp.float32)] if scratch else [],
        compiler_params=pltpu.CompilerParams(vmem_limit_bytes=VMEM_LIMIT),
        cost_estimate=pl.CostEstimate(flops=flops, bytes_accessed=size, transcendentals=0),
        name=name,
    )(*args)


def level_widths(levels, offsets):
    return 0.3 + levels.astype(jnp.float32) * (0.4 / (LEVELS - 1)) + offsets


def surrogate_rows(widths, w_in, b_in, w_out, b_out):
    pre_act = widths[..., None] * w_in + b_in
    hidden = (pre_act * jax.nn.sigmoid(pre_act)).astype(jnp.bfloat16)
    mixed_out = (
        jnp.einsum("rch,hj->jrc", hidden, w_out, preferred_element_type=jnp.float32) + b_out[:, None, None]
    )
    return mixed_out.astype(jnp.bfloat16)


def slope_rows(widths, w_in, b_in, w_out):
    pre_act = widths[..., None] * w_in + b_in
    gate = jax.nn.sigmoid(pre_act)
    slope = gate * (1.0 + pre_act * (1.0 - gate)) * w_in
    return jnp.einsum("rch,hj->jrc", slope.astype(jnp.bfloat16), w_out, preferred_element_type=jnp.float32)


def signed_kappa(index):
    signed = jnp.where(index < SIDE // 2, index, index - SIDE)
    return signed.astype(jnp.float32) * (2.0 * math.pi / SIDE)


def transfer(wavelength, kx, ky, focal_length):
    wave_number = 2.0 * math.pi / wavelength
    kz_square = wave_number * wave_number - kx**2 - ky**2
    kz_root = jnp.sqrt(jnp.abs(kz_square))
    is_open = kz_square > 0.0
    phase_angle = jnp.where(is_open, focal_length * kz_root, 0.0)
    amplitude = jnp.where(is_open, 1.0, jnp.exp(-focal_length * kz_root))
    return (amplitude * jnp.cos(phase_angle), amplitude * jnp.sin(phase_angle))


def usual_transmission(w_in, b_in, w_out, b_out):
    nodes, weights = np.polynomial.hermite_e.hermegauss(8)
    weights = weights / weights.sum()
    shifts = np.clip(0.1 * nodes, -0.3, 0.3)
    places = (0.3 + 0.4 * np.arange(LEVELS)[:, None] / (LEVELS - 1) + shifts[None, :]).reshape(-1)
    shares = np.tile(weights / LEVELS, LEVELS).astype(np.float32)
    pre_act = places.astype(np.float32)[:, None] * w_in[None, :] + b_in[None, :]
    hidden = pre_act * jax.nn.sigmoid(pre_act)
    values = jnp.dot(hidden, w_out.astype(jnp.float32)) + b_out
    mean = jnp.sum(values * shares[:, None], 0)
    spread = jnp.sum((values - mean) ** 2 * shares[:, None], 0)
    return mean, spread


def local(levels, offsets, targets, w_in, b_in, w_out, b_out):
    block = (FIRST, SECOND, LANES)
    packed16 = jax.ShapeDtypeStruct(block, jnp.bfloat16)
    packed32 = jax.ShapeDtypeStruct(block, jnp.float32)
    wave_index = lax.axis_index("z")
    plane_index = lax.axis_index(PLANE)
    wavelength = 1.5 + wave_index.astype(jnp.float32) / (WAVES - 1)
    focal_length = float(SIDE // 16)
    spot_level = float(SIDE // 8)
    forward_cols = jnp.asarray(col_tables(-1.0))
    inverse_cols = jnp.asarray(col_tables(1.0))
    forward_rows = jnp.asarray(row_tables(-1.0))
    inverse_rows = jnp.asarray(row_tables(1.0))
    turns_cols = jnp.asarray(col_twiddles())
    turns_rows = jnp.asarray(row_twiddles())

    widths = level_widths(levels, offsets)
    trans = surrogate_rows(widths, w_in, b_in, w_out, b_out)
    sent = call(pack_kernel, packed16, trans, scratch=False, name="pack")
    cols = lax.all_to_all(sent, SLAB, 0, 0, tiled=True)

    mean, spread = usual_transmission(w_in, b_in, w_out, b_out)
    mean_re = lax.dynamic_index_in_dim(mean, wave_index, 0, keepdims=False)
    mean_im = lax.dynamic_index_in_dim(mean, wave_index + WAVES, 0, keepdims=False)
    noise = lax.dynamic_index_in_dim(spread, wave_index, 0, keepdims=False) + lax.dynamic_index_in_dim(
        spread, wave_index + WAVES, 0, keepdims=False
    )
    zero = jnp.zeros((), jnp.float32)
    dc_re, dc_im = transfer(wavelength, zero, zero, focal_length)
    field_re = mean_re * dc_re - mean_im * dc_im
    field_im = mean_re * dc_im + mean_im * dc_re
    spots_mean = spot_level * targets.shape[1] / (SIDE * SIDE)
    gain = (field_re * field_re + field_im * field_im + 2.0 * noise - spots_mean) / WAVES
    adj_re = gain * field_re
    adj_im = gain * field_im
    back_re = adj_re * dc_re + adj_im * dc_im
    back_im = adj_im * dc_re - adj_re * dc_im
    consts = jnp.stack([mean_re, mean_im, field_re, field_im, adj_re, adj_im, back_re, back_im])
    consts = jnp.broadcast_to(consts[:, None], (8, LANES))

    lane = jnp.arange(LANES, dtype=jnp.int32)
    first = jnp.arange(FIRST, dtype=jnp.int32)
    row = jnp.arange(ROWS, dtype=jnp.int32)[:, None] + ROWS * (lane // SECOND)[None, :]
    kx = signed_kappa(plane_index + FIRST * row)
    ky = signed_kappa(first[:, None] + FIRST * (lane % SECOND)[None, :])
    kern_re, kern_im = transfer(wavelength, kx[None], ky[:, None, :], focal_length)

    own_targets = lax.dynamic_index_in_dim(targets, wave_index, 0, keepdims=False)
    place = (first[:, None] * SECOND + jnp.arange(ROWS, dtype=jnp.int32)[None, :]).reshape(-1)
    row_hits, col_hits = [], []
    for half in range(2):
        row_hits.append(place[:, None] + half * ROWS == own_targets[:, 0][None, :])
        col_hit = own_targets[:, 1][:, None] == (plane_index * SECOND + lane % SECOND)[None, :]
        col_hits.append(col_hit & (lane // SECOND == half)[None, :])
    row_hits = jnp.concatenate(row_hits, 1).astype(jnp.bfloat16)
    col_hits = jnp.concatenate(col_hits, 0).astype(jnp.bfloat16)
    spots = spot_level * jnp.dot(row_hits, col_hits, preferred_element_type=jnp.float32)
    spots = spots.reshape(FIRST, ROWS, LANES)

    slopes = call(pack_kernel, packed32, slope_rows(widths, w_in, b_in, w_out), scratch=False, name="pack_slopes")

    def exchange(x):
        return lax.all_to_all(x, PLANE, 0, 0, tiled=True)

    def filtered(x, conjugate, name):
        kernel = functools.partial(row_kernel, conjugate)
        return call(kernel, packed16, x, kern_re, kern_im, turns_rows, forward_rows, inverse_rows, name=name)

    cols = call(col_first_kernel, packed16, cols, consts, turns_cols, forward_cols, name="col_first")
    rows = filtered(exchange(cols), False, "row_one")
    cols = exchange(rows)
    cols = call(
        col_middle_kernel, packed16, cols, consts, spots, turns_cols, inverse_cols, forward_cols, name="col_middle"
    )
    rows = filtered(exchange(cols), True, "row_two")
    cols = exchange(rows)
    cotangent = call(col_last_kernel, packed16, cols, consts, turns_cols, inverse_cols, name="col_last")
    returned = lax.all_to_all(cotangent, SLAB, 0, 0, tiled=True)
    return call(
        combine_kernel, jax.ShapeDtypeStruct(levels.shape, jnp.float32), returned, slopes, scratch=False, name="combine"
    )


def solution(mesh):
    fine = Mesh(mesh.devices.reshape(2, 4, 2, 8, 2), ("xl", "y", "xh", "z", "c"))
    placed = (P(SLAB, WAVE), P(SLAB, WAVE), P(), P(), P(), P(), P())
    return jax.shard_map(local, mesh=fine, in_specs=placed, out_specs=P(SLAB, WAVE), check_vma=False)
```

```python
import functools
import math

import jax
import jax.numpy as jnp
import ml_dtypes
import numpy as np
from jax import lax
from jax.experimental import pallas as pl
from jax.experimental.pallas import tpu as pltpu
from jax.sharding import Mesh, PartitionSpec as P


LEVELS = 16
WAVES = 8
SIDE = 2048
FIRST = 32
SECOND = 64
LANES = 2 * SECOND
ROWS = SECOND // 2
OUTER = 16
GROUP = 8
SLAB = ("xh", "z", "c")
WAVE = ("xl", "y")
PLANE = ("xh", "c", "xl", "y")
EVERY = ("xh", "z", "c", "xl", "y")
VMEM_LIMIT = 16 * 2**20


def split_np(table):
    high = table.astype(np.float32).astype(ml_dtypes.bfloat16)
    low = (table - high.astype(np.float64)).astype(np.float32).astype(ml_dtypes.bfloat16)
    return high, low


def small_dft(direction):
    place = np.arange(SECOND)
    angle = direction * 2.0 * math.pi / SECOND * (place[:, None] * place[None, :] % SECOND)
    scale = 1.0 if direction < 0 else 1.0 / SIDE
    return np.cos(angle) * scale, np.sin(angle) * scale


def row_tables(direction):
    cos, sin = small_dft(direction)
    pair = np.eye(2)
    table = np.block([[np.kron(pair, cos), np.kron(pair, sin)], [-np.kron(pair, sin), np.kron(pair, cos)]])
    high, low = split_np(table)
    return np.concatenate([high, high, low] if direction < 0 else [high, low], 0)


def col_tables(direction):
    cos, sin = small_dft(direction)
    halves = []
    for cut in (slice(0, ROWS), slice(ROWS, SECOND)):
        halves.append((np.concatenate([cos[:, cut], -sin[:, cut]], 1), np.concatenate([sin[:, cut], cos[:, cut]], 1)))
    high, low = split_np(np.concatenate([halves[0][0], halves[1][0], halves[0][1], halves[1][1]], 0))
    return np.concatenate([high, high, low], 1)


def whole_row_tables(direction):
    place = np.arange(LANES)[:, None]
    freq = np.concatenate([np.arange(0, LANES, 2), np.arange(1, LANES, 2)])[None, :]
    angle = direction * 2.0 * math.pi / LANES * (place * freq % LANES)
    cos, sin = np.cos(angle), np.sin(angle)
    cuts = (slice(0, SECOND), slice(SECOND, LANES))
    if direction < 0:
        table = np.block([[part for cut in cuts for part in (cos[:, cut], sin[:, cut])],
                          [part for cut in cuts for part in (-sin[:, cut], cos[:, cut])]])
        high, low = split_np(table)
        return np.concatenate([high, high, low], 0)
    cos, sin = cos.T / SIDE, sin.T / SIDE
    table = np.concatenate([np.block([[cos[cut], sin[cut]], [-sin[cut], cos[cut]]]) for cut in cuts], 0)
    high, low = split_np(table)
    return np.concatenate([high, low], 0)


def row_twiddles():
    angle = -2.0 * math.pi / SIDE * (np.arange(FIRST)[:, None] * np.arange(SECOND)[None, :])
    return np.stack([np.tile(np.cos(angle), (1, 2)), np.tile(np.sin(angle), (1, 2))], 1).astype(np.float32)


def whole_row_twiddles():
    angle = -2.0 * math.pi / SIDE * (np.arange(OUTER)[:, None] * np.arange(LANES)[None, :])
    return np.stack([np.cos(angle), np.sin(angle)], 1).astype(np.float32)


def col_twiddles():
    place = np.arange(ROWS)[:, None] + ROWS * (np.arange(LANES) // SECOND)[None, :]
    angle = -2.0 * math.pi / SIDE * (np.arange(FIRST)[:, None, None] * place[None])
    return np.stack([np.cos(angle), np.sin(angle)]).astype(np.float32)


def left_lanes():
    return lax.broadcasted_iota(jnp.int32, (1, LANES), 1) < SECOND


def swap(x):
    return pltpu.roll(x, SECOND, x.ndim - 1)


def dft(real, imag, direction):
    count = len(real)
    if count == 1:
        return real, imag
    even_re, even_im = dft(real[0::2], imag[0::2], direction)
    odd_re, odd_im = dft(real[1::2], imag[1::2], direction)
    half = count // 2
    lower_re, lower_im, upper_re, upper_im = [], [], [], []
    for k in range(half):
        a, b = odd_re[k], odd_im[k]
        if k == 0:
            turn_re, turn_im = a, b
        elif 2 * k == half:
            turn_re, turn_im = (b, -a) if direction < 0 else (-b, a)
        else:
            angle = direction * 2.0 * math.pi * k / count
            cos, sin = math.cos(angle), math.sin(angle)
            turn_re, turn_im = a * cos - b * sin, a * sin + b * cos
        lower_re.append(even_re[k] + turn_re)
        lower_im.append(even_im[k] + turn_im)
        upper_re.append(even_re[k] - turn_re)
        upper_im.append(even_im[k] - turn_im)
    return lower_re + upper_re, lower_im + upper_im


def split_pair(x):
    high = x.astype(jnp.bfloat16)
    return high, (x - high.astype(jnp.float32)).astype(jnp.bfloat16)


def matmul(left, right):
    return jnp.dot(left, right, preferred_element_type=jnp.float32)


def load_groups(x_ref, g):
    real = [x_ref[a, g : g + 16, :].astype(jnp.float32) for a in range(FIRST)]
    imag = [x_ref[a, ROWS + g : ROWS + g + 16, :].astype(jnp.float32) for a in range(FIRST)]
    return [([r[h : h + 8] for r in real], [i[h : h + 8] for i in imag]) for h in (0, 8)]


def store_groups(out_ref, g, halves):
    for part in range(2):
        for a in range(FIRST):
            whole = jnp.concatenate([halves[0][part][a], halves[1][part][a]], 0)
            out_ref[a, part * ROWS + g : part * ROWS + g + 16, :] = whole.astype(jnp.bfloat16)


def join_halves(both):
    left = left_lanes()
    parts = []
    for first in (0, 2 * SECOND):
        low, high = both[first : first + SECOND], both[first + SECOND : first + 2 * SECOND]
        base = jnp.where(left, low[:ROWS], high[ROWS:])
        moved = jnp.where(left, low[ROWS:], high[:ROWS])
        parts.append(base + swap(moved))
    return parts


def parts_of(y_ref, rows):
    return [y_ref[0, k, rows, :] for k in range(FIRST)], [y_ref[1, k, rows, :] for k in range(FIRST)]


def turn(real, imag, cos, sin):
    return real * cos - imag * sin, imag * cos + real * sin


def turn_back(real, imag, cos, sin):
    return real * cos + imag * sin, imag * cos - real * sin


def first_kernel(x_ref, a_ref, b_ref, o_ref, m_ref, t_ref, w_ref, out_ref, h_ref, y_ref):
    def block(m, carry):
        for i in range(GROUP):
            tiles = []
            for tile in range(2):
                half = x_ref[m, i : i + 1, tile * LANES : (tile + 1) * LANES] * a_ref[...] + b_ref[...]
                tiles.append((half + half * jnp.tanh(half)).astype(jnp.bfloat16))
            mixed = matmul(o_ref[...], jnp.concatenate(tiles, 1))
            for tile in range(2):
                part = mixed[:, tile * LANES : (tile + 1) * LANES] + m_ref[0]
                part = part.astype(jnp.bfloat16).astype(jnp.float32) - m_ref[1]
                h_ref[2 * m + tile, pl.ds(i, 2 * WAVES, stride=GROUP), :] = part
        return carry

    lax.fori_loop(0, WAVES, block, 0)
    for w in range(WAVES):
        rows_re, rows_im = slice(w * GROUP, (w + 1) * GROUP), slice((WAVES + w) * GROUP, (WAVES + w + 1) * GROUP)
        real, imag = dft(
            [h_ref[a, rows_re, :] for a in range(OUTER)], [h_ref[a, rows_im, :] for a in range(OUTER)], -1.0
        )
        for k in range(OUTER):
            rows = slice((w * OUTER + k) * GROUP, (w * OUTER + k + 1) * GROUP)
            y_ref[rows, :LANES], y_ref[rows, LANES:] = turn(real[k], imag[k], t_ref[k, 0:1, :], t_ref[k, 1:2, :])
    step = 256
    for r in range(0, 1024, step):
        high, low = split_pair(y_ref[r : r + step])
        both = matmul(jnp.concatenate([high, low, high], 1), w_ref[...]).astype(jnp.bfloat16)
        out_ref[r : r + step] = both[:, :LANES]
        out_ref[1024 + r : 1024 + r + step] = both[:, LANES:]


def last_kernel(x_ref, c_ref, d_ref, t_ref, v_ref, out_ref, y_ref):
    step = 256
    for r in range(0, 1024, step):
        data = jnp.concatenate([x_ref[r : r + step], x_ref[1024 + r : 1024 + r + step]], 1)
        y_ref[r : r + step] = matmul(jnp.concatenate([data, data], 1), v_ref[...])
    for a in range(OUTER):
        out_ref[a // 2, :, (a % 2) * LANES : (a % 2 + 1) * LANES] = jnp.zeros((GROUP, LANES), jnp.float32)
    for w in range(WAVES):
        real, imag = [], []
        for k in range(OUTER):
            rows = slice((w * OUTER + k) * GROUP, (w * OUTER + k + 1) * GROUP)
            re, im = turn_back(y_ref[rows, :LANES], y_ref[rows, LANES:], t_ref[k, 0:1, :], t_ref[k, 1:2, :])
            real.append(re)
            imag.append(im)
        real, imag = dft(real, imag, 1.0)
        for a in range(OUTER):
            lanes = slice((a % 2) * LANES, (a % 2 + 1) * LANES)
            total = out_ref[a // 2, :, lanes]
            for j, part in ((w, real[a]), (WAVES + w, imag[a])):
                cotangent = (part + c_ref[j : j + 1, :]).astype(jnp.bfloat16).astype(jnp.float32)
                total = total + cotangent * d_ref[a // 2, j * GROUP : (j + 1) * GROUP, lanes]
            out_ref[a // 2, :, lanes] = total


def load_lanes(x_ref, g):
    left = left_lanes()
    real, imag = [], []
    for a in range(FIRST):
        top = x_ref[a * SECOND + g : a * SECOND + g + 16, :].astype(jnp.float32)
        low = x_ref[a * SECOND + ROWS + g : a * SECOND + ROWS + g + 16, :].astype(jnp.float32)
        real.append(jnp.where(left, top, swap(low)))
        imag.append(jnp.where(left, swap(top), low))
    return [([r[h : h + 8] for r in real], [i[h : h + 8] for i in imag]) for h in (0, 8)]


def store_lanes(out_ref, g, halves):
    left = left_lanes()
    for a in range(FIRST):
        real = jnp.concatenate([halves[0][0][a], halves[1][0][a]], 0)
        imag = jnp.concatenate([halves[0][1][a], halves[1][1][a]], 0)
        top = jnp.where(left, real, swap(imag)).astype(jnp.bfloat16)
        low = jnp.where(left, swap(real), imag).astype(jnp.bfloat16)
        out_ref[a * SECOND + g : a * SECOND + g + 16, :] = top
        out_ref[a * SECOND + ROWS + g : a * SECOND + ROWS + g + 16, :] = low


def col_step(parts, w_ref):
    data = jnp.concatenate([jnp.concatenate(part, 0) for part in parts], 1)
    high, low = split_pair(data)
    both = matmul(w_ref[...], jnp.concatenate([high, low, high], 0))
    return [join_halves(both[:, i * LANES : (i + 1) * LANES]) for i in range(len(parts))]


def col_kernel(conjugate, x_ref, kr_ref, ki_ref, t_ref, w_ref, v_ref, out_ref, y_ref):
    for g in range(0, ROWS, 16):
        halves = load_groups(x_ref, g) if conjugate else load_lanes(x_ref, g)
        for h, (real, imag) in enumerate(halves):
            real, imag = dft(real, imag, -1.0)
            rows = slice(g + 8 * h, g + 8 * h + 8)
            for k in range(FIRST):
                y_ref[0, k, rows, :], y_ref[1, k, rows, :] = turn(
                    real[k], imag[k], t_ref[0, k, rows, :], t_ref[1, k, rows, :]
                )
    for k in range(0, FIRST, 2):
        parts = col_step([(y_ref[0, k + i], y_ref[1, k + i]) for i in range(2)], w_ref)
        for i in range(2):
            turned = turn_back if conjugate else turn
            parts[i] = turned(parts[i][0], parts[i][1], kr_ref[k + i], ki_ref[k + i])
        parts = col_step(parts, v_ref)
        for i in range(2):
            y_ref[0, k + i], y_ref[1, k + i] = turn_back(
                parts[i][0], parts[i][1], t_ref[0, k + i], t_ref[1, k + i]
            )
    for g in range(0, ROWS, 16):
        halves = [dft(*parts_of(y_ref, slice(g + h, g + h + 8)), 1.0) for h in (0, 8)]
        if conjugate:
            store_lanes(out_ref, g, halves)
        else:
            store_groups(out_ref, g, halves)


def middle_kernel(x_ref, c_ref, s_ref, t_ref, v_ref, w_ref, out_ref, y_ref):
    field_re, field_im = c_ref[0:1, :], c_ref[1:2, :]
    mean_re, mean_im = c_ref[2:3, :], c_ref[3:4, :]
    step = 8
    rows = step * ROWS
    for k in range(0, FIRST, step):
        real = jnp.concatenate([x_ref[k + i, :ROWS, :] for i in range(step)], 0)
        imag = jnp.concatenate([x_ref[k + i, ROWS:, :] for i in range(step)], 0)
        both = matmul(jnp.concatenate([real, imag, real, imag], 1), v_ref[...])
        for i in range(step):
            part = slice(i * ROWS, (i + 1) * ROWS)
            y_ref[0, k + i], y_ref[1, k + i] = turn_back(
                both[part, :LANES], both[part, LANES:], t_ref[k + i, 0:1, :], t_ref[k + i, 1:2, :]
            )
    for g in range(0, ROWS, 8):
        part = slice(g, g + 8)
        real, imag = dft(*parts_of(y_ref, part), 1.0)
        for a in range(FIRST):
            value_re, value_im = real[a] + field_re, imag[a] + field_im
            weight = (value_re * value_re + value_im * value_im - s_ref[a, part, :]) * (1.0 / WAVES)
            real[a] = weight * value_re - mean_re
            imag[a] = weight * value_im - mean_im
        real, imag = dft(real, imag, -1.0)
        for k in range(FIRST):
            y_ref[0, k, part, :], y_ref[1, k, part, :] = turn(
                real[k], imag[k], t_ref[k, 0:1, :], t_ref[k, 1:2, :]
            )
    for k in range(0, FIRST, step):
        real = y_ref[0, k : k + step].reshape(rows, LANES)
        imag = y_ref[1, k : k + step].reshape(rows, LANES)
        high, low = split_pair(jnp.concatenate([real, imag], 1))
        both = matmul(jnp.concatenate([high, low, high], 1), w_ref[...]).astype(jnp.bfloat16)
        for i in range(step):
            part = slice(i * ROWS, (i + 1) * ROWS)
            out_ref[k + i] = jnp.concatenate([both[part, :LANES], both[part, LANES:]], 0)


def call(kernel, out_shape, scratch, *args, name=None):
    size = sum(a.size * a.dtype.itemsize for a in args) + math.prod(out_shape.shape) * out_shape.dtype.itemsize
    return pl.pallas_call(
        kernel,
        out_shape=out_shape,
        scratch_shapes=[pltpu.VMEM(shape, jnp.float32) for shape in scratch],
        compiler_params=pltpu.CompilerParams(vmem_limit_bytes=VMEM_LIMIT),
        cost_estimate=pl.CostEstimate(flops=10**8, bytes_accessed=size, transcendentals=0),
        name=name,
    )(*args)


def level_widths(levels, offsets):
    return 0.3 + levels.astype(jnp.float32) * (0.4 / (LEVELS - 1)) + offsets


def slope_rows(widths, w_in, b_in, w_out):
    pre_act = widths[..., None] * w_in + b_in
    gate = jax.nn.sigmoid(pre_act)
    slope = gate * (1.0 + pre_act * (1.0 - gate)) * w_in
    return jnp.einsum("mich,hj->mjic", slope.astype(jnp.bfloat16), w_out, preferred_element_type=jnp.float32)


def signed_kappa(index):
    signed = jnp.where(index < SIDE // 2, index, index - SIDE)
    return signed.astype(jnp.float32) * (2.0 * math.pi / SIDE)


def transfer(wavelength, kx, ky, focal_length):
    wave_number = 2.0 * math.pi / wavelength
    kz_square = wave_number * wave_number - kx**2 - ky**2
    kz_root = jnp.sqrt(jnp.abs(kz_square))
    is_open = kz_square > 0.0
    phase_angle = jnp.where(is_open, focal_length * kz_root, 0.0)
    amplitude = jnp.where(is_open, 1.0, jnp.exp(-focal_length * kz_root))
    return (amplitude * jnp.cos(phase_angle), amplitude * jnp.sin(phase_angle))


def usual_transmission(w_in, b_in, w_out, b_out):
    nodes, weights = np.polynomial.hermite_e.hermegauss(8)
    weights = weights / weights.sum()
    shifts = np.clip(0.1 * nodes, -0.3, 0.3)
    places = (0.3 + 0.4 * np.arange(LEVELS)[:, None] / (LEVELS - 1) + shifts[None, :]).reshape(-1)
    shares = np.tile(weights / LEVELS, LEVELS).astype(np.float32)
    pre_act = places.astype(np.float32)[:, None] * w_in[None, :] + b_in[None, :]
    hidden = pre_act * jax.nn.sigmoid(pre_act)
    values = jnp.dot(hidden, w_out.astype(jnp.float32)) + b_out
    mean = jnp.sum(values * shares[:, None], 0)
    spread = jnp.sum((values - mean) ** 2 * shares[:, None], 0)
    return mean, spread


def local(levels, offsets, targets, w_in, b_in, w_out, b_out):
    block = (FIRST, SECOND, LANES)
    halves = (2, FIRST, ROWS, LANES)
    packed = jax.ShapeDtypeStruct(block, jnp.bfloat16)
    lined = jax.ShapeDtypeStruct((SIDE, LANES), jnp.bfloat16)
    wave_index = lax.axis_index("z")
    plane_index = lax.axis_index(PLANE)
    focal_length = float(SIDE // 16)
    spot_level = float(SIDE // 8)
    forward_cols = jnp.asarray(col_tables(-1.0))
    inverse_cols = jnp.asarray(col_tables(1.0))
    forward_rows = jnp.asarray(row_tables(-1.0))
    inverse_rows = jnp.asarray(row_tables(1.0))
    forward_whole = jnp.asarray(whole_row_tables(-1.0))
    inverse_whole = jnp.asarray(whole_row_tables(1.0))
    turns_cols = jnp.asarray(col_twiddles())
    turns_rows = jnp.asarray(row_twiddles())
    turns_whole = jnp.asarray(whole_row_twiddles())

    rows_here, cols_here = levels.shape
    widths = level_widths(levels, offsets).reshape(WAVES, GROUP, cols_here)
    widths = lax.all_to_all(widths, WAVE, 0, 0, tiled=True)

    mean, spread = usual_transmission(w_in, b_in, w_out, b_out)
    mean_re, mean_im = mean[:WAVES], mean[WAVES:]
    noise = spread[:WAVES] + spread[WAVES:]
    wavelengths = 1.5 + jnp.arange(WAVES, dtype=jnp.int32).astype(jnp.float32) / (WAVES - 1)
    zero = jnp.zeros((), jnp.float32)
    dc_re, dc_im = transfer(wavelengths, zero, zero, focal_length)
    field_re = mean_re * dc_re - mean_im * dc_im
    field_im = mean_re * dc_im + mean_im * dc_re
    spots_mean = spot_level * targets.shape[1] / (SIDE * SIDE)
    gain = (field_re * field_re + field_im * field_im + 2.0 * noise - spots_mean) / WAVES
    adj_re = gain * field_re
    adj_im = gain * field_im
    back = jnp.concatenate([adj_re * dc_re + adj_im * dc_im, adj_im * dc_re - adj_re * dc_im])
    back = jnp.broadcast_to(back[:, None], (2 * WAVES, LANES))
    own = lax.dynamic_index_in_dim(jnp.stack([field_re, field_im, adj_re, adj_im]), wave_index, 1, keepdims=True)
    own = jnp.broadcast_to(own, (4, LANES))
    shifts = jnp.broadcast_to(jnp.stack([b_out, mean])[:, :, None], (2, 2 * WAVES, LANES))

    sent = call(
        first_kernel,
        lined,
        [(OUTER, 2 * WAVES * GROUP, LANES), (1024, 2 * LANES)],
        widths,
        jnp.broadcast_to(0.5 * w_in[:, None], (w_in.shape[0], LANES)),
        jnp.broadcast_to(0.5 * b_in[:, None], (b_in.shape[0], LANES)),
        w_out.T,
        shifts,
        turns_whole,
        forward_whole,
        name="first",
    )
    cols = lax.all_to_all(sent, EVERY, 0, 0, tiled=True)

    lane = jnp.arange(LANES, dtype=jnp.int32)
    first = jnp.arange(FIRST, dtype=jnp.int32)
    row = jnp.arange(ROWS, dtype=jnp.int32)[:, None] + ROWS * (lane // SECOND)[None, :]
    kx = signed_kappa(first[:, None, None] + FIRST * row[None])
    ky = signed_kappa(plane_index + FIRST * (lane % SECOND))
    wavelength = 1.5 + wave_index.astype(jnp.float32) / (WAVES - 1)
    kern_re, kern_im = transfer(wavelength, kx, ky[None, None, :], focal_length)

    own_targets = lax.dynamic_index_in_dim(targets, wave_index, 0, keepdims=False)
    place_row = plane_index * SECOND + jnp.arange(ROWS, dtype=jnp.int32)
    hit_a = own_targets[:, 1][None, :] // SECOND == first[:, None]
    near, far = [], []
    for half in range(2):
        hit_row = own_targets[:, 0][None, :] == (place_row + half * ROWS)[:, None]
        near.append((hit_a[:, None, :] & hit_row[None, :, :]).reshape(FIRST * ROWS, -1))
        hit_col = (own_targets[:, 1] % SECOND)[:, None] == (lane % SECOND)[None, :]
        far.append(hit_col & (lane // SECOND == half)[None, :])
    near = jnp.concatenate(near, 1).astype(jnp.bfloat16)
    far = jnp.concatenate(far, 0).astype(jnp.bfloat16)
    spots = spot_level * jnp.dot(near, far, preferred_element_type=jnp.float32)
    spots = spots.reshape(FIRST, ROWS, LANES)

    slopes = slope_rows(widths, w_in, b_in, w_out).reshape(WAVES, 2 * WAVES * GROUP, cols_here)

    def filtered(x, out_shape, conjugate, name):
        kernel = functools.partial(col_kernel, conjugate)
        return call(
            kernel, out_shape, [halves], x, kern_re, kern_im, turns_cols, forward_cols, inverse_cols, name=name
        )

    def exchange(x):
        return lax.all_to_all(x, PLANE, 0, 0, tiled=True)

    rows = exchange(filtered(cols, packed, False, "filter"))
    rows = call(middle_kernel, packed, [halves], rows, own, spots, turns_rows, inverse_rows, forward_rows, name="middle")
    cols = filtered(exchange(rows), lined, True, "filter_back")
    lines = lax.all_to_all(cols, EVERY, 0, 0, tiled=True)
    gradient = call(
        last_kernel,
        jax.ShapeDtypeStruct((WAVES, GROUP, cols_here), jnp.float32),
        [(1024, 2 * LANES)],
        lines,
        back,
        slopes,
        turns_whole,
        inverse_whole,
        name="last",
    )
    return lax.all_to_all(gradient, WAVE, 0, 0, tiled=True).reshape(rows_here, cols_here)


def solution(mesh):
    fine = Mesh(mesh.devices.reshape(2, 4, 2, 8, 2), ("xl", "y", "xh", "z", "c"))
    placed = (P(SLAB, WAVE), P(SLAB, WAVE), P(), P(), P(), P(), P())
    return jax.shard_map(local, mesh=fine, in_specs=placed, out_specs=P(SLAB, WAVE), check_vma=False)
```

```python
import functools
import math

import jax
import jax.numpy as jnp
import ml_dtypes
import numpy as np
from jax import lax
from jax.experimental import pallas as pl
from jax.experimental.pallas import tpu as pltpu
from jax.sharding import Mesh, PartitionSpec as P


LEVELS = 16
WAVES = 8
SIDE = 2048
FOCAL = 128.0
SPOT_LEVEL = 256.0
SPOTS_MEAN = SPOT_LEVEL * 64 / (SIDE * SIDE)
FIRST = 32
SECOND = 64
LANES = 2 * SECOND
ROWS = SECOND // 2
OUTER = 16
GROUP = 8
SLAB = ("xh", "z", "c")
WAVE = ("xl", "y")
PLANE = ("xh", "c", "xl", "y")
EVERY = ("xh", "z", "c", "xl", "y")
VMEM_LIMIT = 16 * 2**20
COPIES = {'filter': 0, 'middle': 0}
FLOPS = {'prepare': 20000000000, 'first': 100000000, 'filter': 100000000, 'middle': 6000000000, 'spots': 20000000000}


def split_np(table):
    high = table.astype(np.float32).astype(ml_dtypes.bfloat16)
    low = (table - high.astype(np.float64)).astype(np.float32).astype(ml_dtypes.bfloat16)
    return high, low


def small_dft(direction):
    place = np.arange(SECOND)
    angle = direction * 2.0 * math.pi / SECOND * (place[:, None] * place[None, :] % SECOND)
    scale = 1.0 if direction < 0 else 1.0 / SIDE
    return np.cos(angle) * scale, np.sin(angle) * scale


def row_tables(direction):
    cos, sin = small_dft(direction)
    pair = np.eye(2)
    table = np.block([[np.kron(pair, cos), np.kron(pair, sin)], [-np.kron(pair, sin), np.kron(pair, cos)]])
    high, low = split_np(table)
    return np.concatenate([high, high, low] if direction < 0 else [high, low], 0)


def col_tables(direction):
    cos, sin = small_dft(direction)
    halves = []
    for cut in (slice(0, ROWS), slice(ROWS, SECOND)):
        halves.append((np.concatenate([cos[:, cut], -sin[:, cut]], 1), np.concatenate([sin[:, cut], cos[:, cut]], 1)))
    high, low = split_np(np.concatenate([halves[0][0], halves[1][0], halves[0][1], halves[1][1]], 0))
    return np.concatenate([high, high, low], 1)


def whole_row_tables(direction):
    place = np.arange(LANES)[:, None]
    freq = np.concatenate([np.arange(0, LANES, 2), np.arange(1, LANES, 2)])[None, :]
    angle = direction * 2.0 * math.pi / LANES * (place * freq % LANES)
    cos, sin = np.cos(angle), np.sin(angle)
    cuts = (slice(0, SECOND), slice(SECOND, LANES))
    if direction < 0:
        table = np.block([[part for cut in cuts for part in (cos[:, cut], sin[:, cut])],
                          [part for cut in cuts for part in (-sin[:, cut], cos[:, cut])]])
        high, low = split_np(table)
        return np.concatenate([high, high, low], 0)
    cos, sin = cos.T / SIDE, sin.T / SIDE
    table = np.concatenate([np.block([[cos[cut], sin[cut]], [-sin[cut], cos[cut]]]) for cut in cuts], 0)
    high, low = split_np(table)
    return np.concatenate([high, low], 0)


def row_twiddles():
    angle = -2.0 * math.pi / SIDE * (np.arange(FIRST)[:, None] * np.arange(SECOND)[None, :])
    return np.stack([np.tile(np.cos(angle), (1, 2)), np.tile(np.sin(angle), (1, 2))], 1).astype(np.float32)


def whole_row_twiddles():
    angle = -2.0 * math.pi / SIDE * (np.arange(OUTER)[:, None] * np.arange(LANES)[None, :])
    return np.stack([np.cos(angle), np.sin(angle)], 1).astype(np.float32)


def col_twiddles():
    place = np.arange(ROWS)[:, None] + ROWS * (np.arange(LANES) // SECOND)[None, :]
    angle = -2.0 * math.pi / SIDE * (np.arange(FIRST)[:, None, None] * place[None])
    return np.stack([np.cos(angle), np.sin(angle)]).astype(np.float32)


WHOLE_TURN = FIRST


def left_lanes():
    return lax.broadcasted_iota(jnp.int32, (1, LANES), 1) < SECOND


def swap(x):
    return pltpu.roll(x, SECOND, x.ndim - 1)


def dft(real, imag, direction):
    count = len(real)
    if count == 1:
        return real, imag
    even_re, even_im = dft(real[0::2], imag[0::2], direction)
    odd_re, odd_im = dft(real[1::2], imag[1::2], direction)
    half = count // 2
    lower_re, lower_im, upper_re, upper_im = [], [], [], []
    for k in range(half):
        a, b = odd_re[k], odd_im[k]
        if k == 0:
            turn_re, turn_im = a, b
        elif 2 * k == half:
            turn_re, turn_im = (b, -a) if direction < 0 else (-b, a)
        else:
            angle = direction * 2.0 * math.pi * k / count
            cos, sin = math.cos(angle), math.sin(angle)
            turn_re, turn_im = a * cos - b * sin, a * sin + b * cos
        lower_re.append(even_re[k] + turn_re)
        lower_im.append(even_im[k] + turn_im)
        upper_re.append(even_re[k] - turn_re)
        upper_im.append(even_im[k] - turn_im)
    return lower_re + upper_re, lower_im + upper_im


def split_pair(x):
    high = x.astype(jnp.bfloat16)
    return high, (x - high.astype(jnp.float32)).astype(jnp.bfloat16)


def matmul(left, right):
    return jnp.dot(left, right, preferred_element_type=jnp.float32)


class Writer:
    def __init__(self, out_ref, keep):
        self.out_ref = out_ref
        self.keep_ref = keep[0] if keep else out_ref
        self.sems = keep[1] if keep else None
        self.copies = []

    def send(self, *place):
        if self.sems is not None:
            sem = self.sems.at[len(self.copies)]
            copy = pltpu.make_async_copy(self.keep_ref.at[place], self.out_ref.at[place], sem)
            copy.start()
            self.copies.append(copy)

    def wait(self):
        for copy in self.copies:
            copy.wait()


def load_groups(x_ref, g):
    real = [x_ref[a, g : g + 16, :].astype(jnp.float32) for a in range(FIRST)]
    imag = [x_ref[a, ROWS + g : ROWS + g + 16, :].astype(jnp.float32) for a in range(FIRST)]
    return [([r[h : h + 8] for r in real], [i[h : h + 8] for i in imag]) for h in (0, 8)]


def store_groups(out_ref, g, halves):
    for part in range(2):
        for a in range(FIRST):
            whole = jnp.concatenate([halves[0][part][a], halves[1][part][a]], 0)
            out_ref[a, part * ROWS + g : part * ROWS + g + 16, :] = whole.astype(jnp.bfloat16)


def join_halves(both):
    left = left_lanes()
    parts = []
    for first in (0, 2 * SECOND):
        low, high = both[first : first + SECOND], both[first + SECOND : first + 2 * SECOND]
        base = jnp.where(left, low[:ROWS], high[ROWS:])
        moved = jnp.where(left, low[ROWS:], high[:ROWS])
        parts.append(base + swap(moved))
    return parts


def parts_of(y_ref, rows):
    return [y_ref[0, k, rows, :] for k in range(FIRST)], [y_ref[1, k, rows, :] for k in range(FIRST)]


def turn(real, imag, cos, sin):
    return real * cos - imag * sin, imag * cos + real * sin


def turn_back(real, imag, cos, sin):
    return real * cos + imag * sin, imag * cos - real * sin


def column(row):
    return jnp.transpose(jnp.broadcast_to(row, (LANES, row.shape[1])))


def constants_of(values, shares, dc_ref, c_ref):
    mean = jnp.sum(values * shares, axis=1, keepdims=True)
    spread = jnp.sum((values - mean) ** 2 * shares, axis=1, keepdims=True)
    mean = jnp.broadcast_to(mean, (2 * WAVES, LANES))
    mean_re, mean_im = mean[:WAVES], mean[WAVES:]
    noise = jnp.broadcast_to(spread[:WAVES] + spread[WAVES:], (WAVES, LANES))
    dc_re, dc_im = dc_ref[0], dc_ref[1]
    field_re, field_im = turn(mean_re, mean_im, dc_re, dc_im)
    gain = (field_re * field_re + field_im * field_im + 2.0 * noise - SPOTS_MEAN) * (1.0 / WAVES)
    adj_re, adj_im = gain * field_re, gain * field_im
    back = turn_back(adj_re, adj_im, dc_re, dc_im)
    for i, part in enumerate((field_re, field_im, adj_re, adj_im) + back):
        c_ref[i * WAVES : (i + 1) * WAVES, :] = part
    return mean


def prepare_kernel(p_ref, q_ref, b_ref, o_ref, u_ref, dc_ref, s_ref, m_ref, c_ref):
    scale, shift = 0.5 * column(p_ref[...]), 0.5 * column(q_ref[...])
    bias = column(b_ref[...])
    s_ref[0], s_ref[1], m_ref[0] = scale, shift, bias
    half = u_ref[0:1, :] * scale + shift
    usual = matmul(o_ref[...], (half + half * jnp.tanh(half)).astype(jnp.bfloat16)) + bias
    m_ref[1] = constants_of(usual, u_ref[1:2, :], dc_ref, c_ref)


def first_kernel(x_ref, s_ref, m_ref, o_ref, t_ref, w_ref, out_ref, h_ref, y_ref):
    def hidden(row):
        half = row * s_ref[0] + s_ref[1]
        return (half + half * jnp.tanh(half)).astype(jnp.bfloat16)

    for m in range(WAVES):
        for i in range(GROUP):
            tiles = [hidden(x_ref[m, i : i + 1, tile * LANES : (tile + 1) * LANES]) for tile in range(2)]
            mixed = matmul(o_ref[...], jnp.concatenate(tiles, 1))
            for tile in range(2):
                part = mixed[:, tile * LANES : (tile + 1) * LANES] + m_ref[0]
                part = part.astype(jnp.bfloat16).astype(jnp.float32) - m_ref[1]
                h_ref[2 * m + tile, pl.ds(i, 2 * WAVES, stride=GROUP), :] = part
    for w in range(WAVES):
        rows_re, rows_im = slice(w * GROUP, (w + 1) * GROUP), slice((WAVES + w) * GROUP, (WAVES + w + 1) * GROUP)
        real, imag = dft(
            [h_ref[a, rows_re, :] for a in range(OUTER)], [h_ref[a, rows_im, :] for a in range(OUTER)], -1.0
        )
        for k in range(OUTER):
            rows = slice((w * OUTER + k) * GROUP, (w * OUTER + k + 1) * GROUP)
            y_ref[rows, :LANES], y_ref[rows, LANES:] = turn(
                real[k], imag[k], t_ref[WHOLE_TURN + k, 0:1, :], t_ref[WHOLE_TURN + k, 1:2, :]
            )
    step = 256
    for r in range(0, 1024, step):
        high, low = split_pair(y_ref[r : r + step])
        both = matmul(jnp.concatenate([high, low, high], 1), w_ref[...]).astype(jnp.bfloat16)
        for h in range(2):
            rows = slice(h * 1024 + r, h * 1024 + r + step)
            out_ref[rows] = both[:, h * LANES : (h + 1) * LANES]


def last_kernel(x_ref, c_ref, d_ref, t_ref, w_ref, out_ref, y_ref):
    step = 256
    for r in range(0, 1024, step):
        data = jnp.concatenate([x_ref[r : r + step], x_ref[1024 + r : 1024 + r + step]], 1)
        y_ref[r : r + step] = matmul(jnp.concatenate([data, data], 1), w_ref[...])
    for a in range(OUTER):
        out_ref[(a // 2) * GROUP : (a // 2 + 1) * GROUP, (a % 2) * LANES : (a % 2 + 1) * LANES] = jnp.zeros(
            (GROUP, LANES), jnp.float32
        )
    for w in range(WAVES):
        real, imag = [], []
        for k in range(OUTER):
            rows = slice((w * OUTER + k) * GROUP, (w * OUTER + k + 1) * GROUP)
            re, im = turn_back(
                y_ref[rows, :LANES], y_ref[rows, LANES:], t_ref[WHOLE_TURN + k, 0:1, :], t_ref[WHOLE_TURN + k, 1:2, :]
            )
            real.append(re)
            imag.append(im)
        real, imag = dft(real, imag, 1.0)
        for a in range(OUTER):
            lanes = slice((a % 2) * LANES, (a % 2 + 1) * LANES)
            place = slice((a // 2) * GROUP, (a // 2 + 1) * GROUP)
            total = out_ref[place, lanes]
            for j, part in ((w, real[a]), (WAVES + w, imag[a])):
                cotangent = (part + c_ref[4 * WAVES + j : 4 * WAVES + j + 1, :]).astype(jnp.bfloat16).astype(jnp.float32)
                total = total + cotangent * d_ref[a // 2, j * GROUP : (j + 1) * GROUP, lanes]
            out_ref[place, lanes] = total


def load_lanes(x_ref, g):
    left = left_lanes()
    real, imag = [], []
    for a in range(FIRST):
        top = x_ref[a, g : g + 16, :].astype(jnp.float32)
        low = x_ref[a, ROWS + g : ROWS + g + 16, :].astype(jnp.float32)
        real.append(jnp.where(left, top, swap(low)))
        imag.append(jnp.where(left, swap(top), low))
    return [([r[h : h + 8] for r in real], [i[h : h + 8] for i in imag]) for h in (0, 8)]


def store_lanes(out_ref, g, halves):
    left = left_lanes()
    for a in range(FIRST):
        real = jnp.concatenate([halves[0][0][a], halves[1][0][a]], 0)
        imag = jnp.concatenate([halves[0][1][a], halves[1][1][a]], 0)
        out_ref[a, g : g + 16, :] = jnp.where(left, real, swap(imag)).astype(jnp.bfloat16)
        out_ref[a, ROWS + g : ROWS + g + 16, :] = jnp.where(left, swap(real), imag).astype(jnp.bfloat16)


def col_step(parts, table):
    data = jnp.concatenate([jnp.concatenate(part, 0) for part in parts], 1)
    high, low = split_pair(data)
    both = matmul(table, jnp.concatenate([high, low, high], 0))
    return [join_halves(both[:, i * LANES : (i + 1) * LANES]) for i in range(len(parts))]


def col_kernel(conjugate, x_ref, kr_ref, ki_ref, t_ref, w_ref, v_ref, out_ref, y_ref, *keep):
    for g in range(0, ROWS, 16):
        halves = load_groups(x_ref, g) if conjugate else load_lanes(x_ref, g)
        for h, (real, imag) in enumerate(halves):
            real, imag = dft(real, imag, -1.0)
            rows = slice(g + 8 * h, g + 8 * h + 8)
            for k in range(FIRST):
                y_ref[0, k, rows, :], y_ref[1, k, rows, :] = turn(
                    real[k], imag[k], t_ref[0, k, rows, :], t_ref[1, k, rows, :]
                )
    for k in range(0, FIRST, 2):
        parts = col_step([(y_ref[0, k + i], y_ref[1, k + i]) for i in range(2)], w_ref[...])
        for i in range(2):
            turned = turn_back if conjugate else turn
            parts[i] = turned(parts[i][0], parts[i][1], kr_ref[k + i], ki_ref[k + i])
        parts = col_step(parts, v_ref[...])
        for i in range(2):
            y_ref[0, k + i], y_ref[1, k + i] = turn_back(
                parts[i][0], parts[i][1], t_ref[0, k + i], t_ref[1, k + i]
            )
    writer = Writer(out_ref, keep)
    for g in range(0, ROWS, 16):
        halves = [dft(*parts_of(y_ref, slice(g + h, g + h + 8)), 1.0) for h in (0, 8)]
        if conjugate:
            store_lanes(writer.keep_ref, g, halves)
        else:
            store_groups(writer.keep_ref, g, halves)
        for start in (g, ROWS + g):
            place = (slice(None), slice(start, start + 16))
            writer.send(*place)
    writer.wait()


def middle_kernel(x_ref, c_ref, s_ref, t_ref, w_ref, v_ref, out_ref, y_ref, *keep):
    wave = lax.axis_index("z")
    field_re, field_im, mean_re, mean_im = [c_ref[pl.ds(i * WAVES + wave, 1), :] for i in range(4)]
    step = 8
    rows = step * ROWS
    for k in range(0, FIRST, step):
        real = jnp.concatenate([x_ref[k + i, :ROWS, :] for i in range(step)], 0)
        imag = jnp.concatenate([x_ref[k + i, ROWS:, :] for i in range(step)], 0)
        both = matmul(jnp.concatenate([real, imag, real, imag], 1), v_ref[...])
        for i in range(step):
            part = slice(i * ROWS, (i + 1) * ROWS)
            y_ref[0, k + i], y_ref[1, k + i] = turn_back(
                both[part, :LANES], both[part, LANES:], t_ref[k + i, 0:1, :], t_ref[k + i, 1:2, :]
            )
    for g in range(0, ROWS, 8):
        part = slice(g, g + 8)
        real, imag = dft(*parts_of(y_ref, part), 1.0)
        for a in range(FIRST):
            value_re, value_im = real[a] + field_re, imag[a] + field_im
            weight = (value_re * value_re + value_im * value_im - s_ref[a, part, :]) * (1.0 / WAVES)
            real[a] = weight * value_re - mean_re
            imag[a] = weight * value_im - mean_im
        real, imag = dft(real, imag, -1.0)
        for k in range(FIRST):
            y_ref[0, k, part, :], y_ref[1, k, part, :] = turn(
                real[k], imag[k], t_ref[k, 0:1, :], t_ref[k, 1:2, :]
            )
    writer = Writer(out_ref, keep)
    for k in range(0, FIRST, step):
        real = y_ref[0, k : k + step].reshape(rows, LANES)
        imag = y_ref[1, k : k + step].reshape(rows, LANES)
        high, low = split_pair(jnp.concatenate([real, imag], 1))
        both = matmul(jnp.concatenate([high, low, high], 1), w_ref[...]).astype(jnp.bfloat16)
        for i in range(step):
            part = slice(i * ROWS, (i + 1) * ROWS)
            writer.keep_ref[k + i] = jnp.concatenate([both[part, :LANES], both[part, LANES:]], 0)
        writer.send(slice(k, k + step))
    writer.wait()


def spots_kernel(near_ref, far_ref, out_ref):
    out_ref[...] = (SPOT_LEVEL * matmul(near_ref[...], far_ref[...])).reshape(FIRST, ROWS, LANES)


def call(kernel, out_shape, scratch, copies, *args, flops=10**8, size=None, limit=VMEM_LIMIT, name=None):
    outs = out_shape if isinstance(out_shape, tuple) else (out_shape,)
    if size is None:
        size = sum(a.size * a.dtype.itemsize for a in args + outs)
    shapes = [pltpu.VMEM(shape, jnp.float32) for shape in scratch]
    if copies:
        shapes += [pltpu.VMEM(out_shape.shape, out_shape.dtype), pltpu.SemaphoreType.DMA((copies,))]
    where = pl.BlockSpec(memory_space=pltpu.HBM if copies else pltpu.VMEM)
    return pl.pallas_call(
        kernel,
        out_shape=out_shape,
        out_specs=(where,) * len(outs) if isinstance(out_shape, tuple) else where,
        scratch_shapes=shapes,
        compiler_params=pltpu.CompilerParams(vmem_limit_bytes=limit),
        cost_estimate=pl.CostEstimate(flops=flops, bytes_accessed=size, transcendentals=0),
        name=name,
    )(*args)


def level_widths(levels, offsets):
    return 0.3 + levels.astype(jnp.float32) * (0.4 / (LEVELS - 1)) + offsets


def slope_rows(widths, w_in, b_in, w_out):
    pre_act = widths[..., None] * w_in + b_in
    gate = jax.nn.sigmoid(pre_act)
    slope = gate * (1.0 + pre_act * (1.0 - gate)) * w_in
    return jnp.einsum("mich,hj->mjic", slope.astype(jnp.bfloat16), w_out, preferred_element_type=jnp.float32)


def signed_kappa(index):
    signed = jnp.where(index < SIDE // 2, index, index - SIDE)
    return signed.astype(jnp.float32) * (2.0 * math.pi / SIDE)


def transfer(wavelength, kx, ky, focal_length):
    wave_number = 2.0 * math.pi / wavelength
    kz_square = wave_number * wave_number - kx**2 - ky**2
    kz_root = jnp.sqrt(jnp.abs(kz_square))
    is_open = kz_square > 0.0
    phase_angle = jnp.where(is_open, focal_length * kz_root, 0.0)
    amplitude = jnp.where(is_open, 1.0, jnp.exp(-focal_length * kz_root))
    return (amplitude * jnp.cos(phase_angle), amplitude * jnp.sin(phase_angle))


def usual_widths():
    nodes, weights = np.polynomial.hermite_e.hermegauss(8)
    shifts = np.clip(0.1 * nodes, -0.3, 0.3)
    places = (0.3 + 0.4 * np.arange(LEVELS)[:, None] / (LEVELS - 1) + shifts[None, :]).reshape(-1)
    shares = np.tile(weights / weights.sum() / LEVELS, LEVELS)
    return np.stack([places, shares]).astype(np.float32)


def dc_turns():
    angle = FOCAL * 2.0 * math.pi / (1.5 + np.arange(WAVES) / (WAVES - 1))
    turns = np.stack([np.cos(angle), np.sin(angle)]).astype(np.float32)
    return np.ascontiguousarray(np.broadcast_to(turns[:, :, None], (2, WAVES, LANES)))


def local(levels, offsets, targets, w_in, b_in, w_out, b_out):
    block = (FIRST, SECOND, LANES)
    halves = (2, FIRST, ROWS, LANES)
    packed = jax.ShapeDtypeStruct(block, jnp.bfloat16)
    lined = jax.ShapeDtypeStruct((SIDE, LANES), jnp.bfloat16)
    wave_index = lax.axis_index("z")
    plane_index = lax.axis_index(PLANE)
    forward_cols = jnp.asarray(col_tables(-1.0))
    inverse_cols = jnp.asarray(col_tables(1.0))
    forward_rows = jnp.asarray(row_tables(-1.0))
    inverse_rows = jnp.asarray(row_tables(1.0))
    forward_whole = jnp.asarray(whole_row_tables(-1.0))
    inverse_whole = jnp.asarray(whole_row_tables(1.0))
    turns_cols = jnp.asarray(col_twiddles())
    turns_rows = jnp.asarray(np.concatenate([row_twiddles(), whole_row_twiddles()], 0))

    rows_here, cols_here = levels.shape
    widths = lax.all_to_all(level_widths(levels, offsets), WAVE, 0, 0, tiled=True)
    widths = widths.reshape(WAVES, GROUP, cols_here)

    each = 2 * WAVES
    pairs, moments, consts = call(
        prepare_kernel,
        (
            jax.ShapeDtypeStruct((2, w_in.shape[0], LANES), jnp.float32),
            jax.ShapeDtypeStruct((2, each, LANES), jnp.float32),
            jax.ShapeDtypeStruct((3 * each, LANES), jnp.float32),
        ),
        [],
        0,
        w_in.reshape(1, -1),
        b_in.reshape(1, -1),
        b_out.reshape(1, -1),
        w_out.T,
        jnp.asarray(usual_widths()),
        jnp.asarray(dc_turns()),
        flops=FLOPS["prepare"],
        size=0,
        limit=63 * 2**20,
        name="prepare",
    )

    sent = call(
        first_kernel,
        lined,
        [(OUTER, each * GROUP, LANES), (1024, 2 * LANES)],
        0,
        widths,
        pairs,
        moments,
        w_out.T,
        turns_rows,
        forward_whole,
        flops=FLOPS["first"],
        name="first",
    )
    cols = lax.all_to_all(sent, EVERY, 0, 0, tiled=True)

    lane = jnp.arange(LANES, dtype=jnp.int32)
    first = jnp.arange(FIRST, dtype=jnp.int32)
    row = jnp.arange(ROWS, dtype=jnp.int32)[:, None] + ROWS * (lane // SECOND)[None, :]
    kx = signed_kappa(first[:, None, None] + FIRST * row[None])
    ky = signed_kappa(plane_index + FIRST * (lane % SECOND))
    wavelength = 1.5 + wave_index.astype(jnp.float32) / (WAVES - 1)
    kern_re, kern_im = transfer(wavelength, kx, ky[None, None, :], FOCAL)

    own_targets = lax.dynamic_index_in_dim(targets, wave_index, 0, keepdims=False)
    place_row = plane_index * SECOND + jnp.arange(ROWS, dtype=jnp.int32)
    hit_a = own_targets[:, 1][None, :] // SECOND == first[:, None]
    near, far = [], []
    for half in range(2):
        hit_row = own_targets[:, 0][None, :] == (place_row + half * ROWS)[:, None]
        near.append((hit_a[:, None, :] & hit_row[None, :, :]).reshape(FIRST * ROWS, -1))
        hit_col = (own_targets[:, 1] % SECOND)[:, None] == (lane % SECOND)[None, :]
        far.append(hit_col & (lane // SECOND == half)[None, :])
    near = jnp.concatenate(near, 1).astype(jnp.bfloat16)
    far = jnp.concatenate(far, 0).astype(jnp.bfloat16)
    spots = call(
        spots_kernel,
        jax.ShapeDtypeStruct((FIRST, ROWS, LANES), jnp.float32),
        [],
        0,
        near,
        far,
        flops=FLOPS["spots"],
        name="spots",
    )

    slopes = slope_rows(widths, w_in, b_in, w_out).reshape(WAVES, 2 * WAVES * GROUP, cols_here)
    together = (cols, kern_re, kern_im, spots, consts, slopes)
    cols, kern_re, kern_im, spots, consts, slopes = lax.optimization_barrier(together)

    def filtered(x, conjugate, name):
        kernel = functools.partial(col_kernel, conjugate)
        return call(
            kernel,
            packed,
            [halves],
            COPIES["filter"],
            x.reshape(block),
            kern_re,
            kern_im,
            turns_cols,
            forward_cols,
            inverse_cols,
            flops=FLOPS["filter"],
            name=name,
        )

    def exchange(x):
        return lax.all_to_all(x, PLANE, 0, 0, tiled=True)

    rows = exchange(filtered(cols, False, "filter"))
    rows = call(
        middle_kernel,
        packed,
        [halves],
        COPIES["middle"],
        rows,
        consts,
        spots,
        turns_rows,
        forward_rows,
        inverse_rows,
        flops=FLOPS["middle"],
        name="middle",
    )
    cols = filtered(exchange(rows), True, "filter_back").reshape(SIDE, LANES)
    lines = lax.all_to_all(cols, EVERY, 0, 0, tiled=True)
    gradient = call(
        last_kernel,
        jax.ShapeDtypeStruct((rows_here, cols_here), jnp.float32),
        [(1024, 2 * LANES)],
        0,
        lines,
        consts,
        slopes,
        turns_rows,
        inverse_whole,
        name="last",
    )
    return lax.all_to_all(gradient, WAVE, 0, 0, tiled=True)


def solution(mesh):
    fine = Mesh(mesh.devices.reshape(2, 4, 2, 8, 2), ("xl", "y", "xh", "z", "c"))
    placed = (P(SLAB, WAVE), P(SLAB, WAVE), P(), P(), P(), P(), P())
    return jax.shard_map(local, mesh=fine, in_specs=placed, out_specs=P(SLAB, WAVE), check_vma=False)
```

```python
import functools
import math

import jax
import jax.numpy as jnp
import ml_dtypes
import numpy as np
from jax import lax
from jax.experimental import pallas as pl
from jax.experimental.pallas import tpu as pltpu
from jax.sharding import Mesh, PartitionSpec as P


LEVELS = 16
WAVES = 8
SIDE = 2048
FOCAL = 128.0
SPOT_LEVEL = 256.0
SPOTS_MEAN = SPOT_LEVEL * 64 / (SIDE * SIDE)
FIRST = 32
SECOND = 64
LANES = 2 * SECOND
ROWS = SECOND // 2
OUTER = 16
GROUP = 8
SLAB = ("xh", "z", "c")
WAVE = ("xl", "y")
PLANE = ("xh", "c", "xl", "y")
EVERY = ("xh", "z", "c", "xl", "y")
VMEM_LIMIT = 16 * 2**20
COPIES = {'filter': 0, 'middle': 0}
FLOPS = {'prepare': 20000000000, 'first': 100000000, 'filter': 100000000, 'middle': 6000000000, 'spots': 20000000000}


def split_np(table):
    high = table.astype(np.float32).astype(ml_dtypes.bfloat16)
    low = (table - high.astype(np.float64)).astype(np.float32).astype(ml_dtypes.bfloat16)
    return high, low


def small_dft(direction):
    place = np.arange(SECOND)
    angle = direction * 2.0 * math.pi / SECOND * (place[:, None] * place[None, :] % SECOND)
    scale = 1.0 if direction < 0 else 1.0 / SIDE
    return np.cos(angle) * scale, np.sin(angle) * scale


def row_tables(direction):
    cos, sin = small_dft(direction)
    pair = np.eye(2)
    table = np.block([[np.kron(pair, cos), np.kron(pair, sin)], [-np.kron(pair, sin), np.kron(pair, cos)]])
    high, low = split_np(table)
    return np.concatenate([high, high, low] if direction < 0 else [high, low], 0)


def col_tables(direction):
    cos, sin = small_dft(direction)
    halves = []
    for cut in (slice(0, ROWS), slice(ROWS, SECOND)):
        halves.append((np.concatenate([cos[:, cut], -sin[:, cut]], 1), np.concatenate([sin[:, cut], cos[:, cut]], 1)))
    high, low = split_np(np.concatenate([halves[0][0], halves[1][0], halves[0][1], halves[1][1]], 0))
    return np.concatenate([high, high, low], 1)


def whole_row_tables(direction):
    place = np.arange(LANES)[:, None]
    freq = np.concatenate([np.arange(0, LANES, 2), np.arange(1, LANES, 2)])[None, :]
    angle = direction * 2.0 * math.pi / LANES * (place * freq % LANES)
    cos, sin = np.cos(angle), np.sin(angle)
    cuts = (slice(0, SECOND), slice(SECOND, LANES))
    if direction < 0:
        table = np.block([[part for cut in cuts for part in (cos[:, cut], sin[:, cut])],
                          [part for cut in cuts for part in (-sin[:, cut], cos[:, cut])]])
        high, low = split_np(table)
        return np.concatenate([high, high, low], 0)
    cos, sin = cos.T / SIDE, sin.T / SIDE
    table = np.concatenate([np.block([[cos[cut], sin[cut]], [-sin[cut], cos[cut]]]) for cut in cuts], 0)
    high, low = split_np(table)
    return np.concatenate([high, low], 0)


def row_twiddles():
    angle = -2.0 * math.pi / SIDE * (np.arange(FIRST)[:, None] * np.arange(SECOND)[None, :])
    return np.stack([np.tile(np.cos(angle), (1, 2)), np.tile(np.sin(angle), (1, 2))], 1).astype(np.float32)


def whole_row_twiddles():
    angle = -2.0 * math.pi / SIDE * (np.arange(OUTER)[:, None] * np.arange(LANES)[None, :])
    return np.stack([np.cos(angle), np.sin(angle)], 1).astype(np.float32)


def col_twiddles():
    place = np.arange(ROWS)[:, None] + ROWS * (np.arange(LANES) // SECOND)[None, :]
    angle = -2.0 * math.pi / SIDE * (np.arange(FIRST)[:, None, None] * place[None])
    return np.stack([np.cos(angle), np.sin(angle)]).astype(np.float32)


WHOLE_TURN = FIRST


def left_lanes():
    return lax.broadcasted_iota(jnp.int32, (1, LANES), 1) < SECOND


def swap(x):
    return pltpu.roll(x, SECOND, x.ndim - 1)


def dft(real, imag, direction):
    count = len(real)
    if count == 1:
        return real, imag
    even_re, even_im = dft(real[0::2], imag[0::2], direction)
    odd_re, odd_im = dft(real[1::2], imag[1::2], direction)
    half = count // 2
    lower_re, lower_im, upper_re, upper_im = [], [], [], []
    for k in range(half):
        a, b = odd_re[k], odd_im[k]
        if k == 0:
            turn_re, turn_im = a, b
        elif 2 * k == half:
            turn_re, turn_im = (b, -a) if direction < 0 else (-b, a)
        else:
            angle = direction * 2.0 * math.pi * k / count
            cos, sin = math.cos(angle), math.sin(angle)
            turn_re, turn_im = a * cos - b * sin, a * sin + b * cos
        lower_re.append(even_re[k] + turn_re)
        lower_im.append(even_im[k] + turn_im)
        upper_re.append(even_re[k] - turn_re)
        upper_im.append(even_im[k] - turn_im)
    return lower_re + upper_re, lower_im + upper_im


def split_pair(x):
    high = x.astype(jnp.bfloat16)
    return high, (x - high.astype(jnp.float32)).astype(jnp.bfloat16)


def matmul(left, right):
    return jnp.dot(left, right, preferred_element_type=jnp.float32)


class Writer:
    def __init__(self, out_ref, keep):
        self.out_ref = out_ref
        self.keep_ref = keep[0] if keep else out_ref
        self.sems = keep[1] if keep else None
        self.copies = []

    def send(self, *place):
        if self.sems is not None:
            sem = self.sems.at[len(self.copies)]
            copy = pltpu.make_async_copy(self.keep_ref.at[place], self.out_ref.at[place], sem)
            copy.start()
            self.copies.append(copy)

    def wait(self):
        for copy in self.copies:
            copy.wait()


def load_groups(x_ref, g):
    real = [x_ref[a, g : g + 16, :].astype(jnp.float32) for a in range(FIRST)]
    imag = [x_ref[a, ROWS + g : ROWS + g + 16, :].astype(jnp.float32) for a in range(FIRST)]
    return [([r[h : h + 8] for r in real], [i[h : h + 8] for i in imag]) for h in (0, 8)]


def store_groups(out_ref, g, halves):
    for part in range(2):
        for a in range(FIRST):
            whole = jnp.concatenate([halves[0][part][a], halves[1][part][a]], 0)
            out_ref[a, part * ROWS + g : part * ROWS + g + 16, :] = whole.astype(jnp.bfloat16)


def join_halves(both):
    left = left_lanes()
    parts = []
    for first in (0, 2 * SECOND):
        low, high = both[first : first + SECOND], both[first + SECOND : first + 2 * SECOND]
        base = jnp.where(left, low[:ROWS], high[ROWS:])
        moved = jnp.where(left, low[ROWS:], high[:ROWS])
        parts.append(base + swap(moved))
    return parts


def parts_of(y_ref, rows):
    return [y_ref[0, k, rows, :] for k in range(FIRST)], [y_ref[1, k, rows, :] for k in range(FIRST)]


def turn(real, imag, cos, sin):
    return real * cos - imag * sin, imag * cos + real * sin


def turn_back(real, imag, cos, sin):
    return real * cos + imag * sin, imag * cos - real * sin


def column(row):
    return jnp.transpose(jnp.broadcast_to(row, (LANES, row.shape[1])))


def constants_of(values, shares, dc_ref, c_ref):
    mean = jnp.sum(values * shares, axis=1, keepdims=True)
    spread = jnp.sum((values - mean) ** 2 * shares, axis=1, keepdims=True)
    mean = jnp.broadcast_to(mean, (2 * WAVES, LANES))
    mean_re, mean_im = mean[:WAVES], mean[WAVES:]
    noise = jnp.broadcast_to(spread[:WAVES] + spread[WAVES:], (WAVES, LANES))
    dc_re, dc_im = dc_ref[0], dc_ref[1]
    field_re, field_im = turn(mean_re, mean_im, dc_re, dc_im)
    gain = (field_re * field_re + field_im * field_im + 2.0 * noise - SPOTS_MEAN) * (1.0 / WAVES)
    adj_re, adj_im = gain * field_re, gain * field_im
    back = turn_back(adj_re, adj_im, dc_re, dc_im)
    for i, part in enumerate((field_re, field_im, adj_re, adj_im) + back):
        c_ref[i * WAVES : (i + 1) * WAVES, :] = part
    return mean


def prepare_kernel(p_ref, q_ref, b_ref, o_ref, u_ref, dc_ref, s_ref, m_ref, c_ref):
    scale, shift = 0.5 * column(p_ref[...]), 0.5 * column(q_ref[...])
    bias = column(b_ref[...])
    s_ref[0], s_ref[1], m_ref[0] = scale, shift, bias
    half = u_ref[0:1, :] * scale + shift
    usual = matmul(o_ref[...], (half + half * jnp.tanh(half)).astype(jnp.bfloat16)) + bias
    m_ref[1] = constants_of(usual, u_ref[1:2, :], dc_ref, c_ref)


def first_kernel(x_ref, s_ref, m_ref, o_ref, t_ref, w_ref, out_ref, h_ref, y_ref):
    def hidden(row):
        half = row * s_ref[0] + s_ref[1]
        return (half + half * jnp.tanh(half)).astype(jnp.bfloat16)

    for m in range(WAVES):
        for i in range(GROUP):
            tiles = [hidden(x_ref[m, i : i + 1, tile * LANES : (tile + 1) * LANES]) for tile in range(2)]
            mixed = matmul(o_ref[...], jnp.concatenate(tiles, 1))
            for tile in range(2):
                part = mixed[:, tile * LANES : (tile + 1) * LANES] + m_ref[0]
                part = part.astype(jnp.bfloat16).astype(jnp.float32) - m_ref[1]
                h_ref[2 * m + tile, pl.ds(i, 2 * WAVES, stride=GROUP), :] = part
    for w in range(WAVES):
        rows_re, rows_im = slice(w * GROUP, (w + 1) * GROUP), slice((WAVES + w) * GROUP, (WAVES + w + 1) * GROUP)
        real, imag = dft(
            [h_ref[a, rows_re, :] for a in range(OUTER)], [h_ref[a, rows_im, :] for a in range(OUTER)], -1.0
        )
        for k in range(OUTER):
            rows = slice((w * OUTER + k) * GROUP, (w * OUTER + k + 1) * GROUP)
            y_ref[rows, :LANES], y_ref[rows, LANES:] = turn(
                real[k], imag[k], t_ref[WHOLE_TURN + k, 0:1, :], t_ref[WHOLE_TURN + k, 1:2, :]
            )
    step = 256
    for r in range(0, 1024, step):
        high, low = split_pair(y_ref[r : r + step])
        both = matmul(jnp.concatenate([high, low, high], 1), w_ref[...]).astype(jnp.bfloat16)
        for h in range(2):
            rows = slice(h * 1024 + r, h * 1024 + r + step)
            out_ref[rows] = both[:, h * LANES : (h + 1) * LANES]


def last_kernel(x_ref, c_ref, d_ref, t_ref, w_ref, out_ref, y_ref):
    step = 256
    for r in range(0, 1024, step):
        data = jnp.concatenate([x_ref[r : r + step], x_ref[1024 + r : 1024 + r + step]], 1)
        y_ref[r : r + step] = matmul(jnp.concatenate([data, data], 1), w_ref[...])
    for a in range(OUTER):
        out_ref[(a // 2) * GROUP : (a // 2 + 1) * GROUP, (a % 2) * LANES : (a % 2 + 1) * LANES] = jnp.zeros(
            (GROUP, LANES), jnp.float32
        )
    for w in range(WAVES):
        real, imag = [], []
        for k in range(OUTER):
            rows = slice((w * OUTER + k) * GROUP, (w * OUTER + k + 1) * GROUP)
            re, im = turn_back(
                y_ref[rows, :LANES], y_ref[rows, LANES:], t_ref[WHOLE_TURN + k, 0:1, :], t_ref[WHOLE_TURN + k, 1:2, :]
            )
            real.append(re)
            imag.append(im)
        real, imag = dft(real, imag, 1.0)
        for a in range(OUTER):
            lanes = slice((a % 2) * LANES, (a % 2 + 1) * LANES)
            place = slice((a // 2) * GROUP, (a // 2 + 1) * GROUP)
            total = out_ref[place, lanes]
            for j, part in ((w, real[a]), (WAVES + w, imag[a])):
                cotangent = (part + c_ref[4 * WAVES + j : 4 * WAVES + j + 1, :]).astype(jnp.bfloat16).astype(jnp.float32)
                total = total + cotangent * d_ref[a // 2, j * GROUP : (j + 1) * GROUP, lanes]
            out_ref[place, lanes] = total


def load_lanes(x_ref, g):
    left = left_lanes()
    real, imag = [], []
    for a in range(FIRST):
        top = x_ref[a, g : g + 16, :].astype(jnp.float32)
        low = x_ref[a, ROWS + g : ROWS + g + 16, :].astype(jnp.float32)
        real.append(jnp.where(left, top, swap(low)))
        imag.append(jnp.where(left, swap(top), low))
    return [([r[h : h + 8] for r in real], [i[h : h + 8] for i in imag]) for h in (0, 8)]


def store_lanes(out_ref, g, halves):
    left = left_lanes()
    for a in range(FIRST):
        real = jnp.concatenate([halves[0][0][a], halves[1][0][a]], 0)
        imag = jnp.concatenate([halves[0][1][a], halves[1][1][a]], 0)
        out_ref[a, g : g + 16, :] = jnp.where(left, real, swap(imag)).astype(jnp.bfloat16)
        out_ref[a, ROWS + g : ROWS + g + 16, :] = jnp.where(left, swap(real), imag).astype(jnp.bfloat16)


def col_step(parts, table):
    data = jnp.concatenate([jnp.concatenate(part, 0) for part in parts], 1)
    high, low = split_pair(data)
    both = matmul(table, jnp.concatenate([high, low, high], 0))
    return [join_halves(both[:, i * LANES : (i + 1) * LANES]) for i in range(len(parts))]


def col_kernel(conjugate, x_ref, kr_ref, ki_ref, t_ref, w_ref, v_ref, out_ref, y_ref, *keep):
    for g in range(0, ROWS, 16):
        halves = load_groups(x_ref, g) if conjugate else load_lanes(x_ref, g)
        for h, (real, imag) in enumerate(halves):
            real, imag = dft(real, imag, -1.0)
            rows = slice(g + 8 * h, g + 8 * h + 8)
            for k in range(FIRST):
                y_ref[0, k, rows, :], y_ref[1, k, rows, :] = turn(
                    real[k], imag[k], t_ref[0, k, rows, :], t_ref[1, k, rows, :]
                )
    for k in range(0, FIRST, 2):
        parts = col_step([(y_ref[0, k + i], y_ref[1, k + i]) for i in range(2)], w_ref[...])
        for i in range(2):
            turned = turn_back if conjugate else turn
            parts[i] = turned(parts[i][0], parts[i][1], kr_ref[k + i], ki_ref[k + i])
        parts = col_step(parts, v_ref[...])
        for i in range(2):
            y_ref[0, k + i], y_ref[1, k + i] = turn_back(
                parts[i][0], parts[i][1], t_ref[0, k + i], t_ref[1, k + i]
            )
    writer = Writer(out_ref, keep)
    for g in range(0, ROWS, 16):
        halves = [dft(*parts_of(y_ref, slice(g + h, g + h + 8)), 1.0) for h in (0, 8)]
        if conjugate:
            store_lanes(writer.keep_ref, g, halves)
        else:
            store_groups(writer.keep_ref, g, halves)
        for start in (g, ROWS + g):
            place = (slice(None), slice(start, start + 16))
            writer.send(*place)
    writer.wait()


def middle_kernel(x_ref, c_ref, s_ref, t_ref, w_ref, v_ref, out_ref, y_ref, *keep):
    wave = lax.axis_index("z")
    field_re, field_im, mean_re, mean_im = [c_ref[pl.ds(i * WAVES + wave, 1), :] for i in range(4)]
    step = 8
    rows = step * ROWS
    for k in range(0, FIRST, step):
        real = jnp.concatenate([x_ref[k + i, :ROWS, :] for i in range(step)], 0)
        imag = jnp.concatenate([x_ref[k + i, ROWS:, :] for i in range(step)], 0)
        both = matmul(jnp.concatenate([real, imag, real, imag], 1), v_ref[...])
        for i in range(step):
            part = slice(i * ROWS, (i + 1) * ROWS)
            y_ref[0, k + i], y_ref[1, k + i] = turn_back(
                both[part, :LANES], both[part, LANES:], t_ref[k + i, 0:1, :], t_ref[k + i, 1:2, :]
            )
    for g in range(0, ROWS, 8):
        part = slice(g, g + 8)
        real, imag = dft(*parts_of(y_ref, part), 1.0)
        for a in range(FIRST):
            value_re, value_im = real[a] + field_re, imag[a] + field_im
            weight = (value_re * value_re + value_im * value_im - s_ref[a, part, :]) * (1.0 / WAVES)
            real[a] = weight * value_re - mean_re
            imag[a] = weight * value_im - mean_im
        real, imag = dft(real, imag, -1.0)
        for k in range(FIRST):
            y_ref[0, k, part, :], y_ref[1, k, part, :] = turn(
                real[k], imag[k], t_ref[k, 0:1, :], t_ref[k, 1:2, :]
            )
    writer = Writer(out_ref, keep)
    for k in range(0, FIRST, step):
        real = y_ref[0, k : k + step].reshape(rows, LANES)
        imag = y_ref[1, k : k + step].reshape(rows, LANES)
        high, low = split_pair(jnp.concatenate([real, imag], 1))
        both = matmul(jnp.concatenate([high, low, high], 1), w_ref[...]).astype(jnp.bfloat16)
        for i in range(step):
            part = slice(i * ROWS, (i + 1) * ROWS)
            writer.keep_ref[k + i] = jnp.concatenate([both[part, :LANES], both[part, LANES:]], 0)
        writer.send(slice(k, k + step))
    writer.wait()


def spots_kernel(near_ref, far_ref, out_ref):
    out_ref[...] = (SPOT_LEVEL * matmul(near_ref[...], far_ref[...])).reshape(FIRST, ROWS, LANES)


def call(kernel, out_shape, scratch, copies, *args, flops=10**8, size=None, limit=VMEM_LIMIT, name=None):
    outs = out_shape if isinstance(out_shape, tuple) else (out_shape,)
    if size is None:
        size = sum(a.size * a.dtype.itemsize for a in args + outs)
    shapes = [pltpu.VMEM(shape, jnp.float32) for shape in scratch]
    if copies:
        shapes += [pltpu.VMEM(out_shape.shape, out_shape.dtype), pltpu.SemaphoreType.DMA((copies,))]
    where = pl.BlockSpec(memory_space=pltpu.HBM if copies else pltpu.VMEM)
    return pl.pallas_call(
        kernel,
        out_shape=out_shape,
        out_specs=(where,) * len(outs) if isinstance(out_shape, tuple) else where,
        scratch_shapes=shapes,
        compiler_params=pltpu.CompilerParams(vmem_limit_bytes=limit),
        cost_estimate=pl.CostEstimate(flops=flops, bytes_accessed=size, transcendentals=0),
        name=name,
    )(*args)


def level_widths(levels, offsets):
    return 0.3 + levels.astype(jnp.float32) * (0.4 / (LEVELS - 1)) + offsets


def slope_rows(widths, w_in, b_in, w_out):
    pre_act = widths[..., None] * w_in + b_in
    gate = jax.nn.sigmoid(pre_act)
    slope = gate * (1.0 + pre_act * (1.0 - gate)) * w_in
    return jnp.einsum("mich,hj->mjic", slope.astype(jnp.bfloat16), w_out, preferred_element_type=jnp.float32)


def signed_kappa(index):
    signed = jnp.where(index < SIDE // 2, index, index - SIDE)
    return signed.astype(jnp.float32) * (2.0 * math.pi / SIDE)


def transfer(wavelength, kx, ky, focal_length):
    wave_number = 2.0 * math.pi / wavelength
    kz_square = wave_number * wave_number - kx**2 - ky**2
    kz_root = jnp.sqrt(jnp.abs(kz_square))
    is_open = kz_square > 0.0
    phase_angle = jnp.where(is_open, focal_length * kz_root, 0.0)
    amplitude = jnp.where(is_open, 1.0, jnp.exp(-focal_length * kz_root))
    return (amplitude * jnp.cos(phase_angle), amplitude * jnp.sin(phase_angle))


def usual_widths():
    nodes, weights = np.polynomial.hermite_e.hermegauss(8)
    shifts = np.clip(0.1 * nodes, -0.3, 0.3)
    places = (0.3 + 0.4 * np.arange(LEVELS)[:, None] / (LEVELS - 1) + shifts[None, :]).reshape(-1)
    shares = np.tile(weights / weights.sum() / LEVELS, LEVELS)
    return np.stack([places, shares]).astype(np.float32)


def dc_turns():
    angle = FOCAL * 2.0 * math.pi / (1.5 + np.arange(WAVES) / (WAVES - 1))
    turns = np.stack([np.cos(angle), np.sin(angle)]).astype(np.float32)
    return np.ascontiguousarray(np.broadcast_to(turns[:, :, None], (2, WAVES, LANES)))


def local(levels, offsets, targets, w_in, b_in, w_out, b_out):
    block = (FIRST, SECOND, LANES)
    halves = (2, FIRST, ROWS, LANES)
    packed = jax.ShapeDtypeStruct(block, jnp.bfloat16)
    lined = jax.ShapeDtypeStruct((SIDE, LANES), jnp.bfloat16)
    wave_index = lax.axis_index("z")
    plane_index = lax.axis_index(PLANE)
    forward_cols = jnp.asarray(col_tables(-1.0))
    inverse_cols = jnp.asarray(col_tables(1.0))
    forward_rows = jnp.asarray(row_tables(-1.0))
    inverse_rows = jnp.asarray(row_tables(1.0))
    forward_whole = jnp.asarray(whole_row_tables(-1.0))
    inverse_whole = jnp.asarray(whole_row_tables(1.0))
    turns_cols = jnp.asarray(col_twiddles())
    turns_rows = jnp.asarray(np.concatenate([row_twiddles(), whole_row_twiddles()], 0))

    rows_here, cols_here = levels.shape
    widths = lax.all_to_all(level_widths(levels, offsets), WAVE, 0, 0, tiled=True)
    widths = widths.reshape(WAVES, GROUP, cols_here)

    each = 2 * WAVES
    pairs, moments, consts = call(
        prepare_kernel,
        (
            jax.ShapeDtypeStruct((2, w_in.shape[0], LANES), jnp.float32),
            jax.ShapeDtypeStruct((2, each, LANES), jnp.float32),
            jax.ShapeDtypeStruct((3 * each, LANES), jnp.float32),
        ),
        [],
        0,
        w_in.reshape(1, -1),
        b_in.reshape(1, -1),
        b_out.reshape(1, -1),
        w_out.T,
        jnp.asarray(usual_widths()),
        jnp.asarray(dc_turns()),
        flops=FLOPS["prepare"],
        size=0,
        limit=63 * 2**20,
        name="prepare",
    )

    pairs, targets = lax.optimization_barrier((pairs, targets))
    lane = jnp.arange(LANES, dtype=jnp.int32)
    first = jnp.arange(FIRST, dtype=jnp.int32)
    own_targets = lax.dynamic_index_in_dim(targets, wave_index, 0, keepdims=False)
    place_row = plane_index * SECOND + jnp.arange(ROWS, dtype=jnp.int32)
    hit_a = own_targets[:, 1][None, :] // SECOND == first[:, None]
    near, far = [], []
    for half in range(2):
        hit_row = own_targets[:, 0][None, :] == (place_row + half * ROWS)[:, None]
        near.append((hit_a[:, None, :] & hit_row[None, :, :]).reshape(FIRST * ROWS, -1))
        hit_col = (own_targets[:, 1] % SECOND)[:, None] == (lane % SECOND)[None, :]
        far.append(hit_col & (lane // SECOND == half)[None, :])
    near = jnp.concatenate(near, 1).astype(jnp.bfloat16)
    far = jnp.concatenate(far, 0).astype(jnp.bfloat16)
    spots = call(
        spots_kernel,
        jax.ShapeDtypeStruct((FIRST, ROWS, LANES), jnp.float32),
        [],
        0,
        near,
        far,
        flops=FLOPS["spots"],
        name="spots",
    )

    widths, spots = lax.optimization_barrier((widths, spots))

    sent = call(
        first_kernel,
        lined,
        [(OUTER, each * GROUP, LANES), (1024, 2 * LANES)],
        0,
        widths,
        pairs,
        moments,
        w_out.T,
        turns_rows,
        forward_whole,
        flops=FLOPS["first"],
        name="first",
    )
    sent, wave_index, widths = lax.optimization_barrier((sent, wave_index, widths))
    cols = lax.all_to_all(sent, EVERY, 0, 0, tiled=True)

    row = jnp.arange(ROWS, dtype=jnp.int32)[:, None] + ROWS * (lane // SECOND)[None, :]
    kx = signed_kappa(first[:, None, None] + FIRST * row[None])
    ky = signed_kappa(plane_index + FIRST * (lane % SECOND))
    wavelength = 1.5 + wave_index.astype(jnp.float32) / (WAVES - 1)
    kern_re, kern_im = transfer(wavelength, kx, ky[None, None, :], FOCAL)

    slopes = slope_rows(widths, w_in, b_in, w_out).reshape(WAVES, 2 * WAVES * GROUP, cols_here)
    together = (cols, kern_re, kern_im, spots, consts, slopes)
    cols, kern_re, kern_im, spots, consts, slopes = lax.optimization_barrier(together)

    def filtered(x, conjugate, name):
        kernel = functools.partial(col_kernel, conjugate)
        return call(
            kernel,
            packed,
            [halves],
            COPIES["filter"],
            x.reshape(block),
            kern_re,
            kern_im,
            turns_cols,
            forward_cols,
            inverse_cols,
            flops=FLOPS["filter"],
            name=name,
        )

    def exchange(x):
        return lax.all_to_all(x, PLANE, 0, 0, tiled=True)

    rows = exchange(filtered(cols, False, "filter"))
    rows = call(
        middle_kernel,
        packed,
        [halves],
        COPIES["middle"],
        rows,
        consts,
        spots,
        turns_rows,
        forward_rows,
        inverse_rows,
        flops=FLOPS["middle"],
        name="middle",
    )
    cols = filtered(exchange(rows), True, "filter_back").reshape(SIDE, LANES)
    lines = lax.all_to_all(cols, EVERY, 0, 0, tiled=True)
    gradient = call(
        last_kernel,
        jax.ShapeDtypeStruct((rows_here, cols_here), jnp.float32),
        [(1024, 2 * LANES)],
        0,
        lines,
        consts,
        slopes,
        turns_rows,
        inverse_whole,
        name="last",
    )
    return lax.all_to_all(gradient, WAVE, 0, 0, tiled=True)


def solution(mesh):
    fine = Mesh(mesh.devices.reshape(2, 4, 2, 8, 2), ("xl", "y", "xh", "z", "c"))
    placed = (P(SLAB, WAVE), P(SLAB, WAVE), P(), P(), P(), P(), P())
    return jax.shard_map(local, mesh=fine, in_specs=placed, out_specs=P(SLAB, WAVE), check_vma=False)
```

```python
import functools
import math

import jax
import jax.numpy as jnp
import ml_dtypes
import numpy as np
from jax import lax
from jax.experimental import pallas as pl
from jax.experimental.pallas import tpu as pltpu
from jax.sharding import Mesh, PartitionSpec as P


LEVELS = 16
WAVES = 8
SIDE = 2048
FOCAL = 128.0
SPOT_LEVEL = 256.0
SPOTS_MEAN = SPOT_LEVEL * 64 / (SIDE * SIDE)
FIRST = 32
SECOND = 64
LANES = 2 * SECOND
ROWS = SECOND // 2
OUTER = 16
GROUP = 8
SLAB = ("xh", "z", "c")
WAVE = ("xl", "y")
PLANE = ("xh", "c", "xl", "y")
EVERY = ("xh", "z", "c", "xl", "y")
VMEM_LIMIT = 16 * 2**20
COPIES = {'filter': 0, 'middle': 0}
FLOPS = {'prepare': 20000000000, 'first': 100000000, 'filter': 100000000, 'middle': 6000000000, 'spots': 20000000000}


def split_np(table):
    high = table.astype(np.float32).astype(ml_dtypes.bfloat16)
    low = (table - high.astype(np.float64)).astype(np.float32).astype(ml_dtypes.bfloat16)
    return high, low


def small_dft(direction):
    place = np.arange(SECOND)
    angle = direction * 2.0 * math.pi / SECOND * (place[:, None] * place[None, :] % SECOND)
    scale = 1.0 if direction < 0 else 1.0 / SIDE
    return np.cos(angle) * scale, np.sin(angle) * scale


def row_tables(direction):
    cos, sin = small_dft(direction)
    pair = np.eye(2)
    table = np.block([[np.kron(pair, cos), np.kron(pair, sin)], [-np.kron(pair, sin), np.kron(pair, cos)]])
    high, low = split_np(table)
    return np.concatenate([high, high, low] if direction < 0 else [high, low], 0)


def col_tables(direction):
    cos, sin = small_dft(direction)
    halves = []
    for cut in (slice(0, ROWS), slice(ROWS, SECOND)):
        halves.append((np.concatenate([cos[:, cut], -sin[:, cut]], 1), np.concatenate([sin[:, cut], cos[:, cut]], 1)))
    high, low = split_np(np.concatenate([halves[0][0], halves[1][0], halves[0][1], halves[1][1]], 0))
    split = np.concatenate([high, high, low], 1)
    high, low = split_np(np.concatenate([cos, sin], 0))
    return np.concatenate([split, np.concatenate([high, high, low], 1)], 0)


def whole_row_tables(direction):
    place = np.arange(LANES)[:, None]
    freq = np.concatenate([np.arange(0, LANES, 2), np.arange(1, LANES, 2)])[None, :]
    angle = direction * 2.0 * math.pi / LANES * (place * freq % LANES)
    cos, sin = np.cos(angle), np.sin(angle)
    cuts = (slice(0, SECOND), slice(SECOND, LANES))
    if direction < 0:
        table = np.block([[part for cut in cuts for part in (cos[:, cut], sin[:, cut])],
                          [part for cut in cuts for part in (-sin[:, cut], cos[:, cut])]])
        high, low = split_np(table)
        return np.concatenate([high, high, low], 0)
    cos, sin = cos.T / SIDE, sin.T / SIDE
    table = np.concatenate([np.block([[cos[cut], sin[cut]], [-sin[cut], cos[cut]]]) for cut in cuts], 0)
    high, low = split_np(table)
    return np.concatenate([high, low], 0)


def row_twiddles():
    angle = -2.0 * math.pi / SIDE * (np.arange(FIRST)[:, None] * np.arange(SECOND)[None, :])
    return np.stack([np.tile(np.cos(angle), (1, 2)), np.tile(np.sin(angle), (1, 2))], 1).astype(np.float32)


def whole_row_twiddles():
    angle = -2.0 * math.pi / SIDE * (np.arange(OUTER)[:, None] * np.arange(LANES)[None, :])
    return np.stack([np.cos(angle), np.sin(angle)], 1).astype(np.float32)


def col_twiddles():
    place = np.arange(ROWS)[:, None] + ROWS * (np.arange(LANES) // SECOND)[None, :]
    angle = -2.0 * math.pi / SIDE * (np.arange(FIRST)[:, None, None] * place[None])
    return np.stack([np.cos(angle), np.sin(angle)]).astype(np.float32)


WHOLE_TURN = FIRST


def left_lanes():
    return lax.broadcasted_iota(jnp.int32, (1, LANES), 1) < SECOND


def swap(x):
    return pltpu.roll(x, SECOND, x.ndim - 1)


def dft(real, imag, direction):
    count = len(real)
    if count == 1:
        return real, imag
    even_re, even_im = dft(real[0::2], imag[0::2], direction)
    odd_re, odd_im = dft(real[1::2], imag[1::2], direction)
    half = count // 2
    lower_re, lower_im, upper_re, upper_im = [], [], [], []
    for k in range(half):
        a, b = odd_re[k], odd_im[k]
        if k == 0:
            turn_re, turn_im = a, b
        elif 2 * k == half:
            turn_re, turn_im = (b, -a) if direction < 0 else (-b, a)
        else:
            angle = direction * 2.0 * math.pi * k / count
            cos, sin = math.cos(angle), math.sin(angle)
            turn_re, turn_im = a * cos - b * sin, a * sin + b * cos
        lower_re.append(even_re[k] + turn_re)
        lower_im.append(even_im[k] + turn_im)
        upper_re.append(even_re[k] - turn_re)
        upper_im.append(even_im[k] - turn_im)
    return lower_re + upper_re, lower_im + upper_im


def split_pair(x):
    high = x.astype(jnp.bfloat16)
    return high, (x - high.astype(jnp.float32)).astype(jnp.bfloat16)


def matmul(left, right):
    return jnp.dot(left, right, preferred_element_type=jnp.float32)


class Writer:
    def __init__(self, out_ref, keep):
        self.out_ref = out_ref
        self.keep_ref = keep[0] if keep else out_ref
        self.sems = keep[1] if keep else None
        self.copies = []

    def send(self, *place):
        if self.sems is not None:
            sem = self.sems.at[len(self.copies)]
            copy = pltpu.make_async_copy(self.keep_ref.at[place], self.out_ref.at[place], sem)
            copy.start()
            self.copies.append(copy)

    def wait(self):
        for copy in self.copies:
            copy.wait()


def load_groups(x_ref, g):
    real = [x_ref[a, g : g + 16, :].astype(jnp.float32) for a in range(FIRST)]
    imag = [x_ref[a, ROWS + g : ROWS + g + 16, :].astype(jnp.float32) for a in range(FIRST)]
    return [([r[h : h + 8] for r in real], [i[h : h + 8] for i in imag]) for h in (0, 8)]


def store_groups(out_ref, g, halves):
    for part in range(2):
        for a in range(FIRST):
            whole = jnp.concatenate([halves[0][part][a], halves[1][part][a]], 0)
            out_ref[a, part * ROWS + g : part * ROWS + g + 16, :] = whole.astype(jnp.bfloat16)


def join_halves(both):
    left = left_lanes()
    parts = []
    for first in (0, 2 * SECOND):
        low, high = both[first : first + SECOND], both[first + SECOND : first + 2 * SECOND]
        base = jnp.where(left, low[:ROWS], high[ROWS:])
        moved = jnp.where(left, low[ROWS:], high[:ROWS])
        parts.append(base + swap(moved))
    return parts


def parts_of(y_ref, rows):
    return [y_ref[0, k, rows, :] for k in range(FIRST)], [y_ref[1, k, rows, :] for k in range(FIRST)]


def turn(real, imag, cos, sin):
    return real * cos - imag * sin, imag * cos + real * sin


def turn_back(real, imag, cos, sin):
    return real * cos + imag * sin, imag * cos - real * sin


def column(row):
    return jnp.transpose(jnp.broadcast_to(row, (LANES, row.shape[1])))


def constants_of(values, shares, dc_ref, c_ref):
    mean = jnp.sum(values * shares, axis=1, keepdims=True)
    spread = jnp.sum((values - mean) ** 2 * shares, axis=1, keepdims=True)
    mean = jnp.broadcast_to(mean, (2 * WAVES, LANES))
    mean_re, mean_im = mean[:WAVES], mean[WAVES:]
    noise = jnp.broadcast_to(spread[:WAVES] + spread[WAVES:], (WAVES, LANES))
    dc_re, dc_im = dc_ref[0], dc_ref[1]
    field_re, field_im = turn(mean_re, mean_im, dc_re, dc_im)
    gain = (field_re * field_re + field_im * field_im + 2.0 * noise - SPOTS_MEAN) * (1.0 / WAVES)
    adj_re, adj_im = gain * field_re, gain * field_im
    back = turn_back(adj_re, adj_im, dc_re, dc_im)
    for i, part in enumerate((field_re, field_im, adj_re, adj_im) + back):
        c_ref[i * WAVES : (i + 1) * WAVES, :] = part
    return mean


def prepare_kernel(p_ref, q_ref, b_ref, o_ref, u_ref, dc_ref, s_ref, m_ref, c_ref):
    scale, shift = 0.5 * column(p_ref[...]), 0.5 * column(q_ref[...])
    bias = column(b_ref[...])
    s_ref[0], s_ref[1], m_ref[0] = scale, shift, bias
    half = u_ref[0:1, :] * scale + shift
    usual = matmul(o_ref[...], (half + half * jnp.tanh(half)).astype(jnp.bfloat16)) + bias
    m_ref[1] = constants_of(usual, u_ref[1:2, :], dc_ref, c_ref)


def first_kernel(x_ref, s_ref, m_ref, o_ref, t_ref, w_ref, out_ref, h_ref, y_ref):
    def hidden(row):
        half = row * s_ref[0] + s_ref[1]
        return (half + half * jnp.tanh(half)).astype(jnp.bfloat16)

    for m in range(WAVES):
        for i in range(GROUP):
            tiles = [hidden(x_ref[m, i : i + 1, tile * LANES : (tile + 1) * LANES]) for tile in range(2)]
            mixed = matmul(o_ref[...], jnp.concatenate(tiles, 1))
            for tile in range(2):
                part = mixed[:, tile * LANES : (tile + 1) * LANES] + m_ref[0]
                part = part.astype(jnp.bfloat16).astype(jnp.float32) - m_ref[1]
                h_ref[2 * m + tile, pl.ds(i, 2 * WAVES, stride=GROUP), :] = part
    for w in range(WAVES):
        rows_re, rows_im = slice(w * GROUP, (w + 1) * GROUP), slice((WAVES + w) * GROUP, (WAVES + w + 1) * GROUP)
        real, imag = dft(
            [h_ref[a, rows_re, :] for a in range(OUTER)], [h_ref[a, rows_im, :] for a in range(OUTER)], -1.0
        )
        for k in range(OUTER):
            rows = slice((w * OUTER + k) * GROUP, (w * OUTER + k + 1) * GROUP)
            y_ref[rows, :LANES], y_ref[rows, LANES:] = turn(
                real[k], imag[k], t_ref[WHOLE_TURN + k, 0:1, :], t_ref[WHOLE_TURN + k, 1:2, :]
            )
    step = 256
    for r in range(0, 1024, step):
        high, low = split_pair(y_ref[r : r + step])
        both = matmul(jnp.concatenate([high, low, high], 1), w_ref[...]).astype(jnp.bfloat16)
        for h in range(2):
            rows = slice(h * 1024 + r, h * 1024 + r + step)
            out_ref[rows] = both[:, h * LANES : (h + 1) * LANES]


def last_kernel(x_ref, c_ref, d_ref, t_ref, w_ref, out_ref, y_ref):
    step = 256
    for r in range(0, 1024, step):
        data = jnp.concatenate([x_ref[r : r + step], x_ref[1024 + r : 1024 + r + step]], 1)
        y_ref[r : r + step] = matmul(jnp.concatenate([data, data], 1), w_ref[...])
    for a in range(OUTER):
        out_ref[(a // 2) * GROUP : (a // 2 + 1) * GROUP, (a % 2) * LANES : (a % 2 + 1) * LANES] = jnp.zeros(
            (GROUP, LANES), jnp.float32
        )
    for w in range(WAVES):
        real, imag = [], []
        for k in range(OUTER):
            rows = slice((w * OUTER + k) * GROUP, (w * OUTER + k + 1) * GROUP)
            re, im = turn_back(
                y_ref[rows, :LANES], y_ref[rows, LANES:], t_ref[WHOLE_TURN + k, 0:1, :], t_ref[WHOLE_TURN + k, 1:2, :]
            )
            real.append(re)
            imag.append(im)
        real, imag = dft(real, imag, 1.0)
        for a in range(OUTER):
            lanes = slice((a % 2) * LANES, (a % 2 + 1) * LANES)
            place = slice((a // 2) * GROUP, (a // 2 + 1) * GROUP)
            total = out_ref[place, lanes]
            for j, part in ((w, real[a]), (WAVES + w, imag[a])):
                cotangent = (part + c_ref[4 * WAVES + j : 4 * WAVES + j + 1, :]).astype(jnp.bfloat16).astype(jnp.float32)
                total = total + cotangent * d_ref[a // 2, j * GROUP : (j + 1) * GROUP, lanes]
            out_ref[place, lanes] = total


def load_lanes(x_ref, g):
    left = left_lanes()
    real, imag = [], []
    for a in range(FIRST):
        top = x_ref[a, g : g + 16, :].astype(jnp.float32)
        low = x_ref[a, ROWS + g : ROWS + g + 16, :].astype(jnp.float32)
        real.append(jnp.where(left, top, swap(low)))
        imag.append(jnp.where(left, swap(top), low))
    return [([r[h : h + 8] for r in real], [i[h : h + 8] for i in imag]) for h in (0, 8)]


def store_lanes(out_ref, g, halves):
    left = left_lanes()
    for a in range(FIRST):
        real = jnp.concatenate([halves[0][0][a], halves[1][0][a]], 0)
        imag = jnp.concatenate([halves[0][1][a], halves[1][1][a]], 0)
        out_ref[a, g : g + 16, :] = jnp.where(left, real, swap(imag)).astype(jnp.bfloat16)
        out_ref[a, ROWS + g : ROWS + g + 16, :] = jnp.where(left, swap(real), imag).astype(jnp.bfloat16)


def col_step(parts, table):
    data = jnp.concatenate([jnp.concatenate(part, 0) for part in parts], 1)
    high, low = split_pair(data)
    both = matmul(table, jnp.concatenate([high, low, high], 0))
    return [join_halves(both[:, i * LANES : (i + 1) * LANES]) for i in range(len(parts))]


def wide_step(parts, table):
    left = left_lanes()
    data = []
    for real, imag in parts:
        data.append(jnp.concatenate([jnp.where(left, real, swap(imag)), jnp.where(left, swap(real), imag)], 0))
    high, low = split_pair(jnp.concatenate(data, 1))
    both = matmul(table, jnp.concatenate([high, low, high], 0))
    results = []
    for i in range(len(parts)):
        lanes = slice(i * LANES, (i + 1) * LANES)
        c_top, c_low = both[:ROWS, lanes], both[ROWS:SECOND, lanes]
        s_top, s_low = both[SECOND : SECOND + ROWS, lanes], both[SECOND + ROWS :, lanes]
        real = jnp.where(left, c_top, -s_low) + swap(jnp.where(left, c_low, -s_top))
        imag = jnp.where(left, s_top, c_low) + swap(jnp.where(left, s_low, c_top))
        results.append((real, imag))
    return results


def col_kernel(conjugate, x_ref, kr_ref, ki_ref, t_ref, w_ref, v_ref, out_ref, y_ref, *keep):
    for g in range(0, ROWS, 16):
        halves = load_groups(x_ref, g) if conjugate else load_lanes(x_ref, g)
        for h, (real, imag) in enumerate(halves):
            real, imag = dft(real, imag, -1.0)
            rows = slice(g + 8 * h, g + 8 * h + 8)
            for k in range(FIRST):
                y_ref[0, k, rows, :], y_ref[1, k, rows, :] = turn(
                    real[k], imag[k], t_ref[0, k, rows, :], t_ref[1, k, rows, :]
                )
    cut = slice(0, 2 * LANES) if conjugate else slice(2 * LANES, 3 * LANES)
    step = col_step if conjugate else wide_step
    for k in range(0, FIRST, 2):
        parts = step([(y_ref[0, k + i], y_ref[1, k + i]) for i in range(2)], w_ref[cut, :])
        for i in range(2):
            turned = turn_back if conjugate else turn
            parts[i] = turned(parts[i][0], parts[i][1], kr_ref[k + i], ki_ref[k + i])
        parts = step(parts, v_ref[cut, :])
        for i in range(2):
            y_ref[0, k + i], y_ref[1, k + i] = turn_back(
                parts[i][0], parts[i][1], t_ref[0, k + i], t_ref[1, k + i]
            )
    writer = Writer(out_ref, keep)
    for g in range(0, ROWS, 16):
        halves = [dft(*parts_of(y_ref, slice(g + h, g + h + 8)), 1.0) for h in (0, 8)]
        if conjugate:
            store_lanes(writer.keep_ref, g, halves)
        else:
            store_groups(writer.keep_ref, g, halves)
        for start in (g, ROWS + g):
            place = (slice(None), slice(start, start + 16))
            writer.send(*place)
    writer.wait()


def middle_kernel(x_ref, c_ref, s_ref, t_ref, w_ref, v_ref, out_ref, y_ref, *keep):
    wave = lax.axis_index("z")
    field_re, field_im, mean_re, mean_im = [c_ref[pl.ds(i * WAVES + wave, 1), :] for i in range(4)]
    step = 8
    rows = step * ROWS
    for k in range(0, FIRST, step):
        real = jnp.concatenate([x_ref[k + i, :ROWS, :] for i in range(step)], 0)
        imag = jnp.concatenate([x_ref[k + i, ROWS:, :] for i in range(step)], 0)
        both = matmul(jnp.concatenate([real, imag, real, imag], 1), v_ref[...])
        for i in range(step):
            part = slice(i * ROWS, (i + 1) * ROWS)
            y_ref[0, k + i], y_ref[1, k + i] = turn_back(
                both[part, :LANES], both[part, LANES:], t_ref[k + i, 0:1, :], t_ref[k + i, 1:2, :]
            )
    for g in range(0, ROWS, 8):
        part = slice(g, g + 8)
        real, imag = dft(*parts_of(y_ref, part), 1.0)
        for a in range(FIRST):
            value_re, value_im = real[a] + field_re, imag[a] + field_im
            weight = (value_re * value_re + value_im * value_im - s_ref[a, part, :]) * (1.0 / WAVES)
            real[a] = weight * value_re - mean_re
            imag[a] = weight * value_im - mean_im
        real, imag = dft(real, imag, -1.0)
        for k in range(FIRST):
            y_ref[0, k, part, :], y_ref[1, k, part, :] = turn(
                real[k], imag[k], t_ref[k, 0:1, :], t_ref[k, 1:2, :]
            )
    writer = Writer(out_ref, keep)
    for k in range(0, FIRST, step):
        real = y_ref[0, k : k + step].reshape(rows, LANES)
        imag = y_ref[1, k : k + step].reshape(rows, LANES)
        high, low = split_pair(jnp.concatenate([real, imag], 1))
        both = matmul(jnp.concatenate([high, low, high], 1), w_ref[...]).astype(jnp.bfloat16)
        for i in range(step):
            part = slice(i * ROWS, (i + 1) * ROWS)
            writer.keep_ref[k + i] = jnp.concatenate([both[part, :LANES], both[part, LANES:]], 0)
        writer.send(slice(k, k + step))
    writer.wait()


def spots_kernel(near_ref, far_ref, out_ref):
    out_ref[...] = (SPOT_LEVEL * matmul(near_ref[...], far_ref[...])).reshape(FIRST, ROWS, LANES)


def call(kernel, out_shape, scratch, copies, *args, flops=10**8, size=None, limit=VMEM_LIMIT, name=None):
    outs = out_shape if isinstance(out_shape, tuple) else (out_shape,)
    if size is None:
        size = sum(a.size * a.dtype.itemsize for a in args + outs)
    shapes = [pltpu.VMEM(shape, jnp.float32) for shape in scratch]
    if copies:
        shapes += [pltpu.VMEM(out_shape.shape, out_shape.dtype), pltpu.SemaphoreType.DMA((copies,))]
    where = pl.BlockSpec(memory_space=pltpu.HBM if copies else pltpu.VMEM)
    return pl.pallas_call(
        kernel,
        out_shape=out_shape,
        out_specs=(where,) * len(outs) if isinstance(out_shape, tuple) else where,
        scratch_shapes=shapes,
        compiler_params=pltpu.CompilerParams(vmem_limit_bytes=limit),
        cost_estimate=pl.CostEstimate(flops=flops, bytes_accessed=size, transcendentals=0),
        name=name,
    )(*args)


def level_widths(levels, offsets):
    return 0.3 + levels.astype(jnp.float32) * (0.4 / (LEVELS - 1)) + offsets


def slope_rows(widths, w_in, b_in, w_out):
    pre_act = widths[..., None] * w_in + b_in
    gate = jax.nn.sigmoid(pre_act)
    slope = gate * (1.0 + pre_act * (1.0 - gate)) * w_in
    return jnp.einsum("mich,hj->mjic", slope.astype(jnp.bfloat16), w_out, preferred_element_type=jnp.float32)


def signed_kappa(index):
    signed = jnp.where(index < SIDE // 2, index, index - SIDE)
    return signed.astype(jnp.float32) * (2.0 * math.pi / SIDE)


def transfer(wavelength, kx, ky, focal_length):
    wave_number = 2.0 * math.pi / wavelength
    kz_square = wave_number * wave_number - kx**2 - ky**2
    kz_root = jnp.sqrt(jnp.abs(kz_square))
    is_open = kz_square > 0.0
    phase_angle = jnp.where(is_open, focal_length * kz_root, 0.0)
    amplitude = jnp.where(is_open, 1.0, jnp.exp(-focal_length * kz_root))
    return (amplitude * jnp.cos(phase_angle), amplitude * jnp.sin(phase_angle))


def usual_widths():
    nodes, weights = np.polynomial.hermite_e.hermegauss(8)
    shifts = np.clip(0.1 * nodes, -0.3, 0.3)
    places = (0.3 + 0.4 * np.arange(LEVELS)[:, None] / (LEVELS - 1) + shifts[None, :]).reshape(-1)
    shares = np.tile(weights / weights.sum() / LEVELS, LEVELS)
    return np.stack([places, shares]).astype(np.float32)


def dc_turns():
    angle = FOCAL * 2.0 * math.pi / (1.5 + np.arange(WAVES) / (WAVES - 1))
    turns = np.stack([np.cos(angle), np.sin(angle)]).astype(np.float32)
    return np.ascontiguousarray(np.broadcast_to(turns[:, :, None], (2, WAVES, LANES)))


def local(levels, offsets, targets, w_in, b_in, w_out, b_out):
    block = (FIRST, SECOND, LANES)
    halves = (2, FIRST, ROWS, LANES)
    packed = jax.ShapeDtypeStruct(block, jnp.bfloat16)
    lined = jax.ShapeDtypeStruct((SIDE, LANES), jnp.bfloat16)
    wave_index = lax.axis_index("z")
    plane_index = lax.axis_index(PLANE)
    forward_cols = jnp.asarray(col_tables(-1.0))
    inverse_cols = jnp.asarray(col_tables(1.0))
    forward_rows = jnp.asarray(row_tables(-1.0))
    inverse_rows = jnp.asarray(row_tables(1.0))
    forward_whole = jnp.asarray(whole_row_tables(-1.0))
    inverse_whole = jnp.asarray(whole_row_tables(1.0))
    turns_cols = jnp.asarray(col_twiddles())
    turns_rows = jnp.asarray(np.concatenate([row_twiddles(), whole_row_twiddles()], 0))

    rows_here, cols_here = levels.shape
    widths = lax.all_to_all(level_widths(levels, offsets), WAVE, 0, 0, tiled=True)
    widths = widths.reshape(WAVES, GROUP, cols_here)

    each = 2 * WAVES
    pairs, moments, consts = call(
        prepare_kernel,
        (
            jax.ShapeDtypeStruct((2, w_in.shape[0], LANES), jnp.float32),
            jax.ShapeDtypeStruct((2, each, LANES), jnp.float32),
            jax.ShapeDtypeStruct((3 * each, LANES), jnp.float32),
        ),
        [],
        0,
        w_in.reshape(1, -1),
        b_in.reshape(1, -1),
        b_out.reshape(1, -1),
        w_out.T,
        jnp.asarray(usual_widths()),
        jnp.asarray(dc_turns()),
        flops=FLOPS["prepare"],
        size=0,
        limit=63 * 2**20,
        name="prepare",
    )

    pairs, targets = lax.optimization_barrier((pairs, targets))
    lane = jnp.arange(LANES, dtype=jnp.int32)
    first = jnp.arange(FIRST, dtype=jnp.int32)
    own_targets = lax.dynamic_index_in_dim(targets, wave_index, 0, keepdims=False)
    place_row = plane_index * SECOND + jnp.arange(ROWS, dtype=jnp.int32)
    hit_a = own_targets[:, 1][None, :] // SECOND == first[:, None]
    near, far = [], []
    for half in range(2):
        hit_row = own_targets[:, 0][None, :] == (place_row + half * ROWS)[:, None]
        near.append((hit_a[:, None, :] & hit_row[None, :, :]).reshape(FIRST * ROWS, -1))
        hit_col = (own_targets[:, 1] % SECOND)[:, None] == (lane % SECOND)[None, :]
        far.append(hit_col & (lane // SECOND == half)[None, :])
    near = jnp.concatenate(near, 1).astype(jnp.bfloat16)
    far = jnp.concatenate(far, 0).astype(jnp.bfloat16)
    spots = call(
        spots_kernel,
        jax.ShapeDtypeStruct((FIRST, ROWS, LANES), jnp.float32),
        [],
        0,
        near,
        far,
        flops=FLOPS["spots"],
        name="spots",
    )

    widths, spots = lax.optimization_barrier((widths, spots))

    sent = call(
        first_kernel,
        lined,
        [(OUTER, each * GROUP, LANES), (1024, 2 * LANES)],
        0,
        widths,
        pairs,
        moments,
        w_out.T,
        turns_rows,
        forward_whole,
        flops=FLOPS["first"],
        name="first",
    )
    sent, wave_index, widths = lax.optimization_barrier((sent, wave_index, widths))
    cols = lax.all_to_all(sent, EVERY, 0, 0, tiled=True)

    row = jnp.arange(ROWS, dtype=jnp.int32)[:, None] + ROWS * (lane // SECOND)[None, :]
    kx = signed_kappa(first[:, None, None] + FIRST * row[None])
    ky = signed_kappa(plane_index + FIRST * (lane % SECOND))
    wavelength = 1.5 + wave_index.astype(jnp.float32) / (WAVES - 1)
    kern_re, kern_im = transfer(wavelength, kx, ky[None, None, :], FOCAL)

    slopes = slope_rows(widths, w_in, b_in, w_out).reshape(WAVES, 2 * WAVES * GROUP, cols_here)
    together = (cols, kern_re, kern_im, spots, consts, slopes)
    cols, kern_re, kern_im, spots, consts, slopes = lax.optimization_barrier(together)

    def filtered(x, conjugate, name):
        kernel = functools.partial(col_kernel, conjugate)
        return call(
            kernel,
            packed,
            [halves],
            COPIES["filter"],
            x.reshape(block),
            kern_re,
            kern_im,
            turns_cols,
            forward_cols,
            inverse_cols,
            flops=FLOPS["filter"],
            name=name,
        )

    def exchange(x):
        return lax.all_to_all(x, PLANE, 0, 0, tiled=True)

    rows = exchange(filtered(cols, False, "filter"))
    rows = call(
        middle_kernel,
        packed,
        [halves],
        COPIES["middle"],
        rows,
        consts,
        spots,
        turns_rows,
        forward_rows,
        inverse_rows,
        flops=FLOPS["middle"],
        name="middle",
    )
    cols = filtered(exchange(rows), True, "filter_back").reshape(SIDE, LANES)
    lines = lax.all_to_all(cols, EVERY, 0, 0, tiled=True)
    gradient = call(
        last_kernel,
        jax.ShapeDtypeStruct((rows_here, cols_here), jnp.float32),
        [(1024, 2 * LANES)],
        0,
        lines,
        consts,
        slopes,
        turns_rows,
        inverse_whole,
        name="last",
    )
    return lax.all_to_all(gradient, WAVE, 0, 0, tiled=True)


def solution(mesh):
    fine = Mesh(mesh.devices.reshape(2, 4, 2, 8, 2), ("xl", "y", "xh", "z", "c"))
    placed = (P(SLAB, WAVE), P(SLAB, WAVE), P(), P(), P(), P(), P())
    return jax.shard_map(local, mesh=fine, in_specs=placed, out_specs=P(SLAB, WAVE), check_vma=False)
```

```python
import functools
import math

import jax
import jax.numpy as jnp
import ml_dtypes
import numpy as np
from jax import lax
from jax.experimental import pallas as pl
from jax.experimental.pallas import tpu as pltpu
from jax.sharding import Mesh, PartitionSpec as P


LEVELS = 16
WAVES = 8
SIDE = 2048
FOCAL = 128.0
SPOT_LEVEL = 256.0
SPOTS_MEAN = SPOT_LEVEL * 64 / (SIDE * SIDE)
FIRST = 32
SECOND = 64
LANES = 2 * SECOND
ROWS = SECOND // 2
OUTER = 16
GROUP = 8
SLAB = ("xh", "z", "c")
WAVE = ("xl", "y")
PLANE = ("xh", "c", "xl", "y")
EVERY = ("xh", "z", "c", "xl", "y")
VMEM_LIMIT = 16 * 2**20
COPIES = {'filter': 0, 'middle': 0}
FLOPS = {'prepare': 20000000000, 'first': 100000000, 'filter': 100000000, 'middle': 6000000000, 'spots': 20000000000}


def split_np(table):
    high = table.astype(np.float32).astype(ml_dtypes.bfloat16)
    low = (table - high.astype(np.float64)).astype(np.float32).astype(ml_dtypes.bfloat16)
    return high, low


def small_dft(direction):
    place = np.arange(SECOND)
    angle = direction * 2.0 * math.pi / SECOND * (place[:, None] * place[None, :] % SECOND)
    scale = 1.0 if direction < 0 else 1.0 / SIDE
    return np.cos(angle) * scale, np.sin(angle) * scale


def row_tables(direction):
    cos, sin = small_dft(direction)
    pair = np.eye(2)
    table = np.block([[np.kron(pair, cos), np.kron(pair, sin)], [-np.kron(pair, sin), np.kron(pair, cos)]])
    high, low = split_np(table)
    return np.concatenate([high, high, low] if direction < 0 else [high, low], 0)


def col_tables(direction):
    cos, sin = small_dft(direction)
    halves = []
    for cut in (slice(0, ROWS), slice(ROWS, SECOND)):
        halves.append((np.concatenate([cos[:, cut], -sin[:, cut]], 1), np.concatenate([sin[:, cut], cos[:, cut]], 1)))
    high, low = split_np(np.concatenate([halves[0][0], halves[1][0], halves[0][1], halves[1][1]], 0))
    split = np.concatenate([high, high, low], 1)
    high, low = split_np(np.concatenate([cos, sin], 0))
    return np.concatenate([split, np.concatenate([high, high, low], 1)], 0)


def whole_row_tables(direction):
    place = np.arange(LANES)[:, None]
    freq = np.concatenate([np.arange(0, LANES, 2), np.arange(1, LANES, 2)])[None, :]
    angle = direction * 2.0 * math.pi / LANES * (place * freq % LANES)
    cos, sin = np.cos(angle), np.sin(angle)
    cuts = (slice(0, SECOND), slice(SECOND, LANES))
    if direction < 0:
        table = np.block([[part for cut in cuts for part in (cos[:, cut], sin[:, cut])],
                          [part for cut in cuts for part in (-sin[:, cut], cos[:, cut])]])
        high, low = split_np(table)
        return np.concatenate([high, high, low], 0)
    cos, sin = cos.T / SIDE, sin.T / SIDE
    table = np.concatenate([np.block([[cos[cut], sin[cut]], [-sin[cut], cos[cut]]]) for cut in cuts], 0)
    high, low = split_np(table)
    return np.concatenate([high, low], 0)


def row_twiddles():
    angle = -2.0 * math.pi / SIDE * (np.arange(FIRST)[:, None] * np.arange(SECOND)[None, :])
    return np.stack([np.tile(np.cos(angle), (1, 2)), np.tile(np.sin(angle), (1, 2))], 1).astype(np.float32)


def whole_row_twiddles():
    angle = -2.0 * math.pi / SIDE * (np.arange(OUTER)[:, None] * np.arange(LANES)[None, :])
    return np.stack([np.cos(angle), np.sin(angle)], 1).astype(np.float32)


def col_twiddles():
    place = np.arange(ROWS)[:, None] + ROWS * (np.arange(LANES) // SECOND)[None, :]
    angle = -2.0 * math.pi / SIDE * (np.arange(FIRST)[:, None, None] * place[None])
    return np.stack([np.cos(angle), np.sin(angle)]).astype(np.float32)


WHOLE_TURN = FIRST


def left_lanes():
    return lax.broadcasted_iota(jnp.int32, (1, LANES), 1) < SECOND


def swap(x):
    return pltpu.roll(x, SECOND, x.ndim - 1)


def dft(real, imag, direction):
    count = len(real)
    if count == 1:
        return real, imag
    even_re, even_im = dft(real[0::2], imag[0::2], direction)
    odd_re, odd_im = dft(real[1::2], imag[1::2], direction)
    half = count // 2
    lower_re, lower_im, upper_re, upper_im = [], [], [], []
    for k in range(half):
        a, b = odd_re[k], odd_im[k]
        if k == 0:
            turn_re, turn_im = a, b
        elif 2 * k == half:
            turn_re, turn_im = (b, -a) if direction < 0 else (-b, a)
        else:
            angle = direction * 2.0 * math.pi * k / count
            cos, sin = math.cos(angle), math.sin(angle)
            turn_re, turn_im = a * cos - b * sin, a * sin + b * cos
        lower_re.append(even_re[k] + turn_re)
        lower_im.append(even_im[k] + turn_im)
        upper_re.append(even_re[k] - turn_re)
        upper_im.append(even_im[k] - turn_im)
    return lower_re + upper_re, lower_im + upper_im


def split_pair(x):
    high = x.astype(jnp.bfloat16)
    return high, (x - high.astype(jnp.float32)).astype(jnp.bfloat16)


def matmul(left, right):
    return jnp.dot(left, right, preferred_element_type=jnp.float32)


class Writer:
    def __init__(self, out_ref, keep):
        self.out_ref = out_ref
        self.keep_ref = keep[0] if keep else out_ref
        self.sems = keep[1] if keep else None
        self.copies = []

    def send(self, *place):
        if self.sems is not None:
            sem = self.sems.at[len(self.copies)]
            copy = pltpu.make_async_copy(self.keep_ref.at[place], self.out_ref.at[place], sem)
            copy.start()
            self.copies.append(copy)

    def wait(self):
        for copy in self.copies:
            copy.wait()


def load_groups(x_ref, g):
    real = [x_ref[a, g : g + 16, :].astype(jnp.float32) for a in range(FIRST)]
    imag = [x_ref[a, ROWS + g : ROWS + g + 16, :].astype(jnp.float32) for a in range(FIRST)]
    return [([r[h : h + 8] for r in real], [i[h : h + 8] for i in imag]) for h in (0, 8)]


def store_groups(out_ref, g, halves):
    for part in range(2):
        for a in range(FIRST):
            whole = jnp.concatenate([halves[0][part][a], halves[1][part][a]], 0)
            out_ref[a, part * ROWS + g : part * ROWS + g + 16, :] = whole.astype(jnp.bfloat16)


def join_halves(both):
    left = left_lanes()
    parts = []
    for first in (0, 2 * SECOND):
        low, high = both[first : first + SECOND], both[first + SECOND : first + 2 * SECOND]
        base = jnp.where(left, low[:ROWS], high[ROWS:])
        moved = jnp.where(left, low[ROWS:], high[:ROWS])
        parts.append(base + swap(moved))
    return parts


def parts_of(y_ref, rows):
    return [y_ref[0, k, rows, :] for k in range(FIRST)], [y_ref[1, k, rows, :] for k in range(FIRST)]


def turn(real, imag, cos, sin):
    return real * cos - imag * sin, imag * cos + real * sin


def turn_back(real, imag, cos, sin):
    return real * cos + imag * sin, imag * cos - real * sin


def column(row):
    return jnp.transpose(jnp.broadcast_to(row, (LANES, row.shape[1])))


def constants_of(values, shares, dc_ref, c_ref):
    mean = jnp.sum(values * shares, axis=1, keepdims=True)
    spread = jnp.sum((values - mean) ** 2 * shares, axis=1, keepdims=True)
    mean = jnp.broadcast_to(mean, (2 * WAVES, LANES))
    mean_re, mean_im = mean[:WAVES], mean[WAVES:]
    noise = jnp.broadcast_to(spread[:WAVES] + spread[WAVES:], (WAVES, LANES))
    dc_re, dc_im = dc_ref[0], dc_ref[1]
    field_re, field_im = turn(mean_re, mean_im, dc_re, dc_im)
    gain = (field_re * field_re + field_im * field_im + 2.0 * noise - SPOTS_MEAN) * (1.0 / WAVES)
    adj_re, adj_im = gain * field_re, gain * field_im
    back = turn_back(adj_re, adj_im, dc_re, dc_im)
    for i, part in enumerate((field_re, field_im, adj_re, adj_im) + back):
        c_ref[i * WAVES : (i + 1) * WAVES, :] = part
    return mean


def prepare_kernel(p_ref, q_ref, b_ref, o_ref, u_ref, dc_ref, s_ref, m_ref, c_ref):
    scale, shift = 0.5 * column(p_ref[...]), 0.5 * column(q_ref[...])
    bias = column(b_ref[...])
    s_ref[0], s_ref[1], m_ref[0] = scale, shift, bias
    half = u_ref[0:1, :] * scale + shift
    usual = matmul(o_ref[...], (half + half * jnp.tanh(half)).astype(jnp.bfloat16)) + bias
    m_ref[1] = constants_of(usual, u_ref[1:2, :], dc_ref, c_ref)


def first_kernel(x_ref, s_ref, m_ref, o_ref, t_ref, w_ref, out_ref, h_ref, y_ref):
    def hidden(row):
        half = row * s_ref[0] + s_ref[1]
        return (half + half * jnp.tanh(half)).astype(jnp.bfloat16)

    for m in range(WAVES):
        for i in range(GROUP):
            tiles = [hidden(x_ref[m, i : i + 1, tile * LANES : (tile + 1) * LANES]) for tile in range(2)]
            mixed = matmul(o_ref[...], jnp.concatenate(tiles, 1))
            for tile in range(2):
                part = mixed[:, tile * LANES : (tile + 1) * LANES] + m_ref[0]
                part = part.astype(jnp.bfloat16).astype(jnp.float32) - m_ref[1]
                h_ref[2 * m + tile, pl.ds(i, 2 * WAVES, stride=GROUP), :] = part
    for w in range(WAVES):
        rows_re, rows_im = slice(w * GROUP, (w + 1) * GROUP), slice((WAVES + w) * GROUP, (WAVES + w + 1) * GROUP)
        real, imag = dft(
            [h_ref[a, rows_re, :] for a in range(OUTER)], [h_ref[a, rows_im, :] for a in range(OUTER)], -1.0
        )
        for k in range(OUTER):
            rows = slice((w * OUTER + k) * GROUP, (w * OUTER + k + 1) * GROUP)
            y_ref[rows, :LANES], y_ref[rows, LANES:] = turn(
                real[k], imag[k], t_ref[WHOLE_TURN + k, 0:1, :], t_ref[WHOLE_TURN + k, 1:2, :]
            )
    step = 256
    for r in range(0, 1024, step):
        high, low = split_pair(y_ref[r : r + step])
        both = matmul(jnp.concatenate([high, low, high], 1), w_ref[...]).astype(jnp.bfloat16)
        for h in range(2):
            rows = slice(h * 1024 + r, h * 1024 + r + step)
            out_ref[rows] = both[:, h * LANES : (h + 1) * LANES]


def last_kernel(x_ref, c_ref, d_ref, t_ref, w_ref, out_ref, y_ref):
    step = 256
    for r in range(0, 1024, step):
        data = jnp.concatenate([x_ref[r : r + step], x_ref[1024 + r : 1024 + r + step]], 1)
        y_ref[r : r + step] = matmul(jnp.concatenate([data, data], 1), w_ref[...])
    for a in range(OUTER):
        out_ref[(a // 2) * GROUP : (a // 2 + 1) * GROUP, (a % 2) * LANES : (a % 2 + 1) * LANES] = jnp.zeros(
            (GROUP, LANES), jnp.float32
        )
    for w in range(WAVES):
        real, imag = [], []
        for k in range(OUTER):
            rows = slice((w * OUTER + k) * GROUP, (w * OUTER + k + 1) * GROUP)
            re, im = turn_back(
                y_ref[rows, :LANES], y_ref[rows, LANES:], t_ref[WHOLE_TURN + k, 0:1, :], t_ref[WHOLE_TURN + k, 1:2, :]
            )
            real.append(re)
            imag.append(im)
        real, imag = dft(real, imag, 1.0)
        for a in range(OUTER):
            lanes = slice((a % 2) * LANES, (a % 2 + 1) * LANES)
            place = slice((a // 2) * GROUP, (a // 2 + 1) * GROUP)
            total = out_ref[place, lanes]
            for j, part in ((w, real[a]), (WAVES + w, imag[a])):
                cotangent = (part + c_ref[4 * WAVES + j : 4 * WAVES + j + 1, :]).astype(jnp.bfloat16).astype(jnp.float32)
                total = total + cotangent * d_ref[a // 2, j * GROUP : (j + 1) * GROUP, lanes]
            out_ref[place, lanes] = total


def load_lanes(x_ref, g):
    left = left_lanes()
    real, imag = [], []
    for a in range(FIRST):
        top = x_ref[a, g : g + 16, :].astype(jnp.float32)
        low = x_ref[a, ROWS + g : ROWS + g + 16, :].astype(jnp.float32)
        real.append(jnp.where(left, top, swap(low)))
        imag.append(jnp.where(left, swap(top), low))
    return [([r[h : h + 8] for r in real], [i[h : h + 8] for i in imag]) for h in (0, 8)]


def store_lanes(out_ref, g, halves):
    left = left_lanes()
    for a in range(FIRST):
        real = jnp.concatenate([halves[0][0][a], halves[1][0][a]], 0)
        imag = jnp.concatenate([halves[0][1][a], halves[1][1][a]], 0)
        out_ref[a, g : g + 16, :] = jnp.where(left, real, swap(imag)).astype(jnp.bfloat16)
        out_ref[a, ROWS + g : ROWS + g + 16, :] = jnp.where(left, swap(real), imag).astype(jnp.bfloat16)


def col_step(parts, table):
    data = jnp.concatenate([jnp.concatenate(part, 0) for part in parts], 1)
    high, low = split_pair(data)
    both = matmul(table, jnp.concatenate([high, low, high], 0))
    return [join_halves(both[:, i * LANES : (i + 1) * LANES]) for i in range(len(parts))]


def wide_step(parts, table):
    left = left_lanes()
    data = []
    for real, imag in parts:
        data.append(jnp.concatenate([jnp.where(left, real, swap(imag)), jnp.where(left, swap(real), imag)], 0))
    high, low = split_pair(jnp.concatenate(data, 1))
    both = matmul(table, jnp.concatenate([high, low, high], 0))
    results = []
    for i in range(len(parts)):
        lanes = slice(i * LANES, (i + 1) * LANES)
        c_top, c_low = both[:ROWS, lanes], both[ROWS:SECOND, lanes]
        s_top, s_low = both[SECOND : SECOND + ROWS, lanes], both[SECOND + ROWS :, lanes]
        real = jnp.where(left, c_top, -s_low) + swap(jnp.where(left, c_low, -s_top))
        imag = jnp.where(left, s_top, c_low) + swap(jnp.where(left, s_low, c_top))
        results.append((real, imag))
    return results


def col_kernel(conjugate, x_ref, kr_ref, ki_ref, t_ref, w_ref, v_ref, out_ref, y_ref, *keep):
    for g in range(0, ROWS, 16):
        halves = load_groups(x_ref, g) if conjugate else load_lanes(x_ref, g)
        for h, (real, imag) in enumerate(halves):
            real, imag = dft(real, imag, -1.0)
            rows = slice(g + 8 * h, g + 8 * h + 8)
            for k in range(FIRST):
                y_ref[0, k, rows, :], y_ref[1, k, rows, :] = turn(
                    real[k], imag[k], t_ref[0, k, rows, :], t_ref[1, k, rows, :]
                )
    cut = slice(0, 2 * LANES) if conjugate else slice(2 * LANES, 3 * LANES)
    step = col_step if conjugate else wide_step
    for k in range(0, FIRST, 2):
        parts = step([(y_ref[0, k + i], y_ref[1, k + i]) for i in range(2)], w_ref[cut, :])
        for i in range(2):
            turned = turn_back if conjugate else turn
            parts[i] = turned(parts[i][0], parts[i][1], kr_ref[k + i], ki_ref[k + i])
        parts = step(parts, v_ref[cut, :])
        for i in range(2):
            y_ref[0, k + i], y_ref[1, k + i] = turn_back(
                parts[i][0], parts[i][1], t_ref[0, k + i], t_ref[1, k + i]
            )
    writer = Writer(out_ref, keep)
    for g in range(0, ROWS, 16):
        halves = [dft(*parts_of(y_ref, slice(g + h, g + h + 8)), 1.0) for h in (0, 8)]
        if conjugate:
            store_lanes(writer.keep_ref, g, halves)
        else:
            store_groups(writer.keep_ref, g, halves)
        for start in (g, ROWS + g):
            place = (slice(None), slice(start, start + 16))
            writer.send(*place)
    writer.wait()


def middle_kernel(x_ref, c_ref, s_ref, t_ref, w_ref, v_ref, out_ref, y_ref, *keep):
    wave = lax.axis_index("z")
    field_re, field_im, mean_re, mean_im = [c_ref[pl.ds(i * WAVES + wave, 1), :] for i in range(4)]
    step = 8
    rows = step * ROWS
    for k in range(0, FIRST, step):
        real = jnp.concatenate([x_ref[k + i, :ROWS, :] for i in range(step)], 0)
        imag = jnp.concatenate([x_ref[k + i, ROWS:, :] for i in range(step)], 0)
        both = matmul(jnp.concatenate([real, imag, real, imag], 1), v_ref[...])
        for i in range(step):
            part = slice(i * ROWS, (i + 1) * ROWS)
            y_ref[0, k + i], y_ref[1, k + i] = turn_back(
                both[part, :LANES], both[part, LANES:], t_ref[k + i, 0:1, :], t_ref[k + i, 1:2, :]
            )
    for g in range(0, ROWS, 8):
        part = slice(g, g + 8)
        real, imag = dft(*parts_of(y_ref, part), 1.0)
        for a in range(FIRST):
            value_re, value_im = real[a] + field_re, imag[a] + field_im
            weight = (value_re * value_re + value_im * value_im - s_ref[a, part, :]) * (1.0 / WAVES)
            real[a] = weight * value_re - mean_re
            imag[a] = weight * value_im - mean_im
        real, imag = dft(real, imag, -1.0)
        for k in range(FIRST):
            y_ref[0, k, part, :], y_ref[1, k, part, :] = turn(
                real[k], imag[k], t_ref[k, 0:1, :], t_ref[k, 1:2, :]
            )
    writer = Writer(out_ref, keep)
    for k in range(0, FIRST, step):
        real = y_ref[0, k : k + step].reshape(rows, LANES)
        imag = y_ref[1, k : k + step].reshape(rows, LANES)
        high, low = split_pair(jnp.concatenate([real, imag], 1))
        both = matmul(jnp.concatenate([high, low, high], 1), w_ref[...]).astype(jnp.bfloat16)
        for i in range(step):
            part = slice(i * ROWS, (i + 1) * ROWS)
            writer.keep_ref[k + i] = jnp.concatenate([both[part, :LANES], both[part, LANES:]], 0)
        writer.send(slice(k, k + step))
    writer.wait()


def spots_kernel(near_ref, far_ref, out_ref):
    out_ref[...] = (SPOT_LEVEL * matmul(near_ref[...], far_ref[...])).reshape(FIRST, ROWS, LANES)


def call(kernel, out_shape, scratch, copies, *args, flops=10**8, size=None, limit=VMEM_LIMIT, name=None):
    outs = out_shape if isinstance(out_shape, tuple) else (out_shape,)
    if size is None:
        size = sum(a.size * a.dtype.itemsize for a in args + outs)
    shapes = [pltpu.VMEM(shape, jnp.float32) for shape in scratch]
    if copies:
        shapes += [pltpu.VMEM(out_shape.shape, out_shape.dtype), pltpu.SemaphoreType.DMA((copies,))]
    where = pl.BlockSpec(memory_space=pltpu.HBM if copies else pltpu.VMEM)
    return pl.pallas_call(
        kernel,
        out_shape=out_shape,
        out_specs=(where,) * len(outs) if isinstance(out_shape, tuple) else where,
        scratch_shapes=shapes,
        compiler_params=pltpu.CompilerParams(vmem_limit_bytes=limit),
        cost_estimate=pl.CostEstimate(flops=flops, bytes_accessed=size, transcendentals=0),
        name=name,
    )(*args)


def level_widths(levels, offsets):
    return 0.3 + levels.astype(jnp.float32) * (0.4 / (LEVELS - 1)) + offsets


def slope_rows(widths, w_in, b_in, w_out):
    pre_act = widths[..., None] * w_in + b_in
    gate = jax.nn.sigmoid(pre_act)
    slope = gate * (1.0 + pre_act * (1.0 - gate)) * w_in
    return jnp.einsum("mich,hj->mjic", slope.astype(jnp.bfloat16), w_out, preferred_element_type=jnp.float32)


def signed_kappa(index):
    signed = jnp.where(index < SIDE // 2, index, index - SIDE)
    return signed.astype(jnp.float32) * (2.0 * math.pi / SIDE)


def transfer(wavelength, kx, ky, focal_length):
    wave_number = 2.0 * math.pi / wavelength
    kz_square = wave_number * wave_number - kx**2 - ky**2
    kz_root = jnp.sqrt(jnp.abs(kz_square))
    is_open = kz_square > 0.0
    phase_angle = jnp.where(is_open, focal_length * kz_root, 0.0)
    amplitude = jnp.where(is_open, 1.0, jnp.exp(-focal_length * kz_root))
    return (amplitude * jnp.cos(phase_angle), amplitude * jnp.sin(phase_angle))


def usual_widths():
    nodes, weights = np.polynomial.hermite_e.hermegauss(8)
    shifts = np.clip(0.1 * nodes, -0.3, 0.3)
    places = (0.3 + 0.4 * np.arange(LEVELS)[:, None] / (LEVELS - 1) + shifts[None, :]).reshape(-1)
    shares = np.tile(weights / weights.sum() / LEVELS, LEVELS)
    return np.stack([places, shares]).astype(np.float32)


def dc_turns():
    angle = FOCAL * 2.0 * math.pi / (1.5 + np.arange(WAVES) / (WAVES - 1))
    turns = np.stack([np.cos(angle), np.sin(angle)]).astype(np.float32)
    return np.ascontiguousarray(np.broadcast_to(turns[:, :, None], (2, WAVES, LANES)))


def local(levels, offsets, targets, w_in, b_in, w_out, b_out):
    block = (FIRST, SECOND, LANES)
    halves = (2, FIRST, ROWS, LANES)
    packed = jax.ShapeDtypeStruct(block, jnp.bfloat16)
    lined = jax.ShapeDtypeStruct((SIDE, LANES), jnp.bfloat16)
    wave_index = lax.axis_index("z")
    plane_index = lax.axis_index(PLANE)
    forward_cols = jnp.asarray(col_tables(-1.0))
    inverse_cols = jnp.asarray(col_tables(1.0))
    forward_rows = jnp.asarray(row_tables(-1.0))
    inverse_rows = jnp.asarray(row_tables(1.0))
    forward_whole = jnp.asarray(whole_row_tables(-1.0))
    inverse_whole = jnp.asarray(whole_row_tables(1.0))
    turns_cols = jnp.asarray(col_twiddles())
    turns_rows = jnp.asarray(np.concatenate([row_twiddles(), whole_row_twiddles()], 0))

    rows_here, cols_here = levels.shape
    widths = lax.all_to_all(level_widths(levels, offsets), WAVE, 0, 0, tiled=True)
    widths = widths.reshape(WAVES, GROUP, cols_here)

    each = 2 * WAVES
    pairs, moments, consts = call(
        prepare_kernel,
        (
            jax.ShapeDtypeStruct((2, w_in.shape[0], LANES), jnp.float32),
            jax.ShapeDtypeStruct((2, each, LANES), jnp.float32),
            jax.ShapeDtypeStruct((3 * each, LANES), jnp.float32),
        ),
        [],
        0,
        w_in.reshape(1, -1),
        b_in.reshape(1, -1),
        b_out.reshape(1, -1),
        w_out.T,
        jnp.asarray(usual_widths()),
        jnp.asarray(dc_turns()),
        flops=FLOPS["prepare"],
        size=0,
        limit=63 * 2**20,
        name="prepare",
    )

    pairs, targets = lax.optimization_barrier((pairs, targets))
    lane = jnp.arange(LANES, dtype=jnp.int32)
    first = jnp.arange(FIRST, dtype=jnp.int32)
    own_targets = lax.dynamic_index_in_dim(targets, wave_index, 0, keepdims=False)
    near_row = own_targets[:, 0] - plane_index * SECOND
    held = (near_row >= 0) & (near_row < SECOND)
    code = jnp.where(held, own_targets[:, 1] // SECOND * SECOND + near_row, -1)
    place = (first[:, None] * SECOND + jnp.arange(ROWS, dtype=jnp.int32)[None, :]).reshape(-1)
    half = lane // SECOND
    near = (place[:, None] + ROWS * half[None, :] == jnp.tile(code, 2)[None, :]).astype(jnp.bfloat16)
    spot_lane = jnp.tile(own_targets[:, 1] % SECOND, 2) + SECOND * half
    far = (spot_lane[:, None] == lane[None, :]).astype(jnp.bfloat16)
    spots = call(
        spots_kernel,
        jax.ShapeDtypeStruct((FIRST, ROWS, LANES), jnp.float32),
        [],
        0,
        near,
        far,
        flops=FLOPS["spots"],
        name="spots",
    )

    widths, spots = lax.optimization_barrier((widths, spots))

    sent = call(
        first_kernel,
        lined,
        [(OUTER, each * GROUP, LANES), (1024, 2 * LANES)],
        0,
        widths,
        pairs,
        moments,
        w_out.T,
        turns_rows,
        forward_whole,
        flops=FLOPS["first"],
        name="first",
    )
    sent, wave_index, widths = lax.optimization_barrier((sent, wave_index, widths))
    cols = lax.all_to_all(sent, EVERY, 0, 0, tiled=True)

    row = jnp.arange(ROWS, dtype=jnp.int32)[:, None] + ROWS * (lane // SECOND)[None, :]
    kx = signed_kappa(first[:, None, None] + FIRST * row[None])
    ky = signed_kappa(plane_index + FIRST * (lane % SECOND))
    wavelength = 1.5 + wave_index.astype(jnp.float32) / (WAVES - 1)
    kern_re, kern_im = transfer(wavelength, kx, ky[None, None, :], FOCAL)

    slopes = slope_rows(widths, w_in, b_in, w_out).reshape(WAVES, 2 * WAVES * GROUP, cols_here)
    together = (cols, kern_re, kern_im, spots, consts, slopes)
    cols, kern_re, kern_im, spots, consts, slopes = lax.optimization_barrier(together)

    def filtered(x, conjugate, name):
        kernel = functools.partial(col_kernel, conjugate)
        return call(
            kernel,
            packed,
            [halves],
            COPIES["filter"],
            x.reshape(block),
            kern_re,
            kern_im,
            turns_cols,
            forward_cols,
            inverse_cols,
            flops=FLOPS["filter"],
            name=name,
        )

    def exchange(x):
        return lax.all_to_all(x, PLANE, 0, 0, tiled=True)

    rows = exchange(filtered(cols, False, "filter"))
    rows = call(
        middle_kernel,
        packed,
        [halves],
        COPIES["middle"],
        rows,
        consts,
        spots,
        turns_rows,
        forward_rows,
        inverse_rows,
        flops=FLOPS["middle"],
        name="middle",
    )
    cols = filtered(exchange(rows), True, "filter_back").reshape(SIDE, LANES)
    lines = lax.all_to_all(cols, EVERY, 0, 0, tiled=True)
    gradient = call(
        last_kernel,
        jax.ShapeDtypeStruct((rows_here, cols_here), jnp.float32),
        [(1024, 2 * LANES)],
        0,
        lines,
        consts,
        slopes,
        turns_rows,
        inverse_whole,
        name="last",
    )
    return lax.all_to_all(gradient, WAVE, 0, 0, tiled=True)


def solution(mesh):
    fine = Mesh(mesh.devices.reshape(2, 4, 2, 8, 2), ("xl", "y", "xh", "z", "c"))
    placed = (P(SLAB, WAVE), P(SLAB, WAVE), P(), P(), P(), P(), P())
    return jax.shard_map(local, mesh=fine, in_specs=placed, out_specs=P(SLAB, WAVE), check_vma=False)
```
